128 devices in a mesh: pole: 4 (over z_hi, core), snode: 32 (over x, z_lo, y).
Axes of the slice: x: 4, y: 4, z: 4 (z_hi: 2, z_lo: 2; z = z_hi * 2 + z_lo), core: 2. Of those that a mesh axis runs over, the one named last changes fastest.
Arguments:
- root_inverse: bfloat16 [4, 2, 96, 12288, 128], P('pole', None, None, 'snode'), may hold values from -6 to 6
- factor_columns: bfloat16 [4, 32, 2, 1024, 128], P('pole', 'snode'), may hold values from -0.1875 to 0.1875
- diagonal_inverse: bfloat16 [4, 32, 2, 128, 128], P('pole', 'snode'), may hold values from -6 to 6
- pattern: int32 [32, 8], replicated, may hold values from 0 to 95, all different within a row
- pole_weights: float32 [4, 2], P('pole'), may hold values from -4 to 4
- pole_shifts: float32 [4, 2], P('pole'), may hold values from -2 to 2
Outputs:
- density_rows: float32 [2, 32, 32, 384, 128], P(None, 'snode', None, 'pole')
- density_diagonal: float32 [2, 32, 128, 128], P(None, 'snode', 'pole')
The draws below stay inside these ranges and needn't reach their ends.
Inputs may be any that keep to these rules, and one draw needn't show every extreme that they name: Each row of pattern lists 8 different root blocks; every root block is listed by some row.
All inputs are finite; a program needn't handle non-finite values.
Results may differ from the reference program's by a relative error of at most 0.0029.
Values may be sent and summed in bfloat16 or wider, within the bound.
No kernel may reach another device: no remote copies, remote signals or barrier semaphores. Data moves between devices by JAX's collectives and lax.ppermute only.
A program may use at most 448 MiB of HBM per device.

```python
import jax
import jax.numpy as jnp
from jax import lax

B = 128
M = 8
RB_DEV = 3
POLES = 4
NS = 32
RB = 96
NR = 12288
N_SNODE = 32


def level_of(rng, extent, pieces, low, high):
    gain, own = 1.0, jax.random.fold_in(rng, 6)
    for position, shards_of in pieces:
        draws = jnp.exp(jax.random.uniform(jax.random.fold_in(own, position), (shards_of,), jnp.float32, low / len(pieces), high / len(pieces)))
        gain = gain * jnp.repeat(draws, extent[position] // shards_of).reshape([-1 if axis == position else 1 for axis in range(len(extent))])
    return gain


def different_ones(own_key, rows, amount, top, lift):
    order = jax.random.permutation(jax.random.fold_in(own_key, 1), amount)
    favour = order
    for power in range(3):
        favour = favour * favour // amount
    favour = favour * lift // amount
    chance = jax.random.randint(jax.random.fold_in(own_key, 2), (rows, amount), 0, 4096) + favour
    fixed_rows = jax.random.permutation(jax.random.fold_in(own_key, 3), rows)[jnp.arange(amount) % rows]
    chance = jnp.where(jnp.arange(rows)[:, None] == fixed_rows[None, :], 1 << 14, chance)
    score = chance * amount + jnp.arange(amount)
    return lax.top_k(score.astype(jnp.int32), top)[1].astype(jnp.int32)


def bell_draw(stream_key, shape, width, reach, shards=(), held_as=jnp.bfloat16):
    array = width * jax.random.normal(stream_key, shape, jnp.float32)
    if shards:
        array = array * level_of(stream_key, shape, shards, -0.22, 0.18)
    return jnp.clip(array, -reach, reach).astype(held_as)


def setup_inputs(seed: int = 0) -> dict:
    streams_of = jax.random.split(jax.random.key(seed), 7)
    return {
        "root_inverse": bell_draw(streams_of[0], (POLES, 2, RB, NR, B), 1.0, 6.0, ((0, 4), (3, 32))),
        "factor_columns": bell_draw(streams_of[1], (POLES, NS, 2, M * B, B), (M * B) ** -0.5, 0.1875, ((0, 4), (1, 32))),
        "diagonal_inverse": bell_draw(streams_of[2], (POLES, NS, 2, B, B), 1.0, 6.0, ((0, 4), (1, 32))),
        "pattern": different_ones(streams_of[3], NS, RB, M, 1365),
        "pole_weights": bell_draw(streams_of[4], (POLES, 2), 1.0, 4.0, ((0, 4),), jnp.float32),
        "pole_shifts": jnp.clip(jax.random.uniform(streams_of[5], (POLES, 2), jnp.float32, -2.0, 2.0) * level_of(streams_of[5], (POLES, 2), ((0, 4),), -0.4, 0.0), -2.0, 2.0),
    }


def complex_dot(left_real, left_imag, right_real, right_imag):
    left_real = left_real.astype(jnp.float32)
    left_imag = left_imag.astype(jnp.float32)
    right_real = right_real.astype(jnp.float32)
    right_imag = right_imag.astype(jnp.float32)
    real_part = jnp.dot(left_real, right_real, preferred_element_type=jnp.float32) - jnp.dot(left_imag, right_imag, preferred_element_type=jnp.float32)
    imag_part = jnp.dot(left_real, right_imag, preferred_element_type=jnp.float32) + jnp.dot(left_imag, right_real, preferred_element_type=jnp.float32)
    return real_part, imag_part


def imaginary(coef_real, coef_imag, value_real, value_imag):
    return coef_real * value_imag + coef_imag * value_real


def reference(root_inverse, factor_columns, diagonal_inverse, pattern, pole_weights, pole_shifts):
    total_rows = RB * B
    rho_rows = jnp.zeros((NS, total_rows, B), jnp.float32)
    energy_rows = jnp.zeros((NS, total_rows, B), jnp.float32)
    rho_diag = jnp.zeros((NS, B, B), jnp.float32)
    energy_diag = jnp.zeros((NS, B, B), jnp.float32)
    for pole in range(POLES):
        blocks = root_inverse[pole]

        def one_node(operands):
            block_ids, factor, diag_inv = operands
            chosen = jnp.take(blocks, block_ids, axis=1)
            chosen = jnp.transpose(chosen, (0, 2, 1, 3)).reshape(2, total_rows, M * B)
            real_part, imag_part = complex_dot(chosen[0], chosen[1], factor[0], factor[1])
            column = jnp.stack([-real_part, -imag_part]).astype(jnp.bfloat16)
            picked = jnp.take(column.reshape(2, RB, B, B), block_ids, axis=1).reshape(2, M * B, B)
            sum_real, sum_imag = complex_dot(factor[0].T, factor[1].T, picked[0], picked[1])
            diagonal = jnp.stack([diag_inv[0].astype(jnp.float32) - sum_real, diag_inv[1].astype(jnp.float32) - sum_imag])
            return column, diagonal

        columns, diagonals = lax.map(one_node, (pattern, factor_columns[pole], diagonal_inverse[pole]))
        weight_real = pole_weights[pole, 0]
        weight_imag = pole_weights[pole, 1]
        shift_real = pole_shifts[pole, 0]
        shift_imag = pole_shifts[pole, 1]
        energy_real = weight_real * shift_real - weight_imag * shift_imag
        energy_imag = weight_real * shift_imag + weight_imag * shift_real
        column_values = columns.astype(jnp.float32)
        rho_rows = rho_rows + imaginary(weight_real, weight_imag, column_values[:, 0], column_values[:, 1])
        energy_rows = energy_rows + imaginary(energy_real, energy_imag, column_values[:, 0], column_values[:, 1])
        rho_diag = rho_diag + imaginary(weight_real, weight_imag, diagonals[:, 0], diagonals[:, 1])
        energy_diag = energy_diag + imaginary(energy_real, energy_imag, diagonals[:, 0], diagonals[:, 1])
    density_rows = jnp.stack([rho_rows, energy_rows]).reshape(2, NS, N_SNODE, RB_DEV * B, B)
    density_diagonal = jnp.stack([rho_diag, energy_diag])
    return density_rows, density_diagonal
```

```python
import jax
import jax.numpy as jnp
from jax import lax
from jax.experimental import pallas as pl
from jax.experimental.pallas import tpu as pltpu
from jax.sharding import PartitionSpec as P

B = 128
M = 8
ROWS = 384
PART = 96
DIAG = 32
SX, SZ, SY = 4, 2, 4
NODES = SX * SZ * SY
NEAR = (0, 1, -1)
RING = (0, 1, -1, 2)
CORE = [(p, p ^ 1) for p in range(4)]
Z_HI = [(p, p ^ 2) for p in range(4)]
INNER = [(dx, dy) for dx in NEAR for dy in NEAR]
OUTER = [(2, dy) for dy in RING] + [(dx, 2) for dx in NEAR]


def shift(dx=0, dz=0, dy=0):
    return [
        (
            (x * SZ + z) * SY + y,
            (((x + dx) % SX) * SZ + (z + dz) % SZ) * SY + (y + dy) % SY,
        )
        for x in range(SX)
        for z in range(SZ)
        for y in range(SY)
    ]


def send(value, **by):
    return lax.ppermute(value, "snode", shift(**by))


def ring(first, second, axis):
    up, down = {axis: 1}, {axis: -1}
    below = (send(first, **up), send(second, **up))
    above = (send(first, **down), send(second, **down))
    far = (send(below[0], **up), send(above[1], **down))
    return {0: (first, second), 1: above, -1: below, 2: far}


def gathered(factor):
    quarter = [factor[:, q * 256 : (q + 1) * 256] for q in range(4)]
    along_x = ring(quarter[0], quarter[1], "dx")
    along_y = ring(quarter[2], quarter[3], "dy")
    left = [jnp.stack([along_x[d][h] for d in RING]) for h in range(2)]
    right = [jnp.stack([along_y[d][h] for d in RING]) for h in range(2)]
    return ring(left[0], left[1], "dy"), ring(right[0], right[1], "dx")


def column_body(places, own_at, meta, root, diag_inv, *refs):
    count = len(places)
    n_src = 1 + max(src for place in places for src, _ in place)
    sources = refs[:n_src]
    outs = refs[n_src : n_src + 4]
    blocks, factors, column, total, root_sem, factor_sem = refs[n_src + 4 :]
    for j, place in enumerate(places):
        for q, (src, at) in enumerate(place):
            pltpu.make_async_copy(sources[src].at[at], factors.at[j, q], factor_sem.at[j]).start()

        for i in range(M):
            block = meta[j * M + i]
            for h in range(2):
                pltpu.make_async_copy(
                    root.at[0, h, block],
                    blocks.at[j, :, pl.ds((2 * i + h) * B, B)],
                    root_sem.at[j],
                ).start()
    first_block = meta[count * M]
    pole = meta[count * M + 1]

    @pl.loop(0, count)
    def _(j):
        pltpu.make_async_copy(factors.at[j], factors.at[j], factor_sem.at[j]).wait()
        pltpu.make_async_copy(blocks.at[j], blocks.at[j], root_sem.at[j]).wait()
        weights = []
        for i in range(M):
            at = pl.ds((i % 2) * B, B)
            real, imag = factors[j, i // 2, 0, at, :], factors[j, i // 2, 1, at, :]
            weights.append(jnp.concatenate([real, imag], axis=1))
            weights.append(jnp.concatenate([-imag, real], axis=1))
        product = jnp.dot(
            blocks[j], jnp.concatenate(weights, axis=0), preferred_element_type=jnp.float32
        )
        column[...] = (-product).astype(jnp.bfloat16)
        total[...] = jnp.zeros_like(total)
        for i in range(M):
            local = meta[j * M + i] - first_block

            @pl.when((local >= 0) & (local < ROWS // B))
            def _():
                rows = column[pl.ds(pl.multiple_of(local * B, B), B), :]
                real, imag = rows[:, :B], rows[:, B:]
                values = jnp.concatenate(
                    [
                        jnp.concatenate([real, imag], axis=1),
                        jnp.concatenate([-imag, real], axis=1),
                    ],
                    axis=0,
                )
                at = pl.ds((i % 2) * B, B)
                left = jnp.concatenate(
                    [factors[j, i // 2, 0, at, :], factors[j, i // 2, 1, at, :]], axis=0
                )
                total[...] += lax.dot_general(
                    left, values, (((0,), (0,)), ((), ())), preferred_element_type=jnp.float32
                )

        if own_at is not None:

            @pl.when(j == own_at)
            def _():
                total[:, :B] -= diag_inv[0].astype(jnp.float32)
                total[:, B:] -= diag_inv[1].astype(jnp.float32)

        for n, out in enumerate(outs):
            part = pole ^ (((n & 1) << 1) | (n >> 1))
            rows_at = pl.multiple_of(part * PART, PART)
            diag_at = pl.multiple_of(part * DIAG, DIAG)
            for h in range(2):
                lanes = slice(h * B, (h + 1) * B)
                out[j, h, :PART, :] = column[pl.ds(rows_at, PART), lanes]
                share = -total[pl.ds(diag_at, DIAG), lanes]
                coarse = share.astype(jnp.bfloat16)
                out[j, h, PART : PART + DIAG, :] = coarse
                rest = share - coarse.astype(jnp.float32)
                out[j, h, PART + DIAG :, :] = rest.astype(jnp.bfloat16)


def columns_of(places, own_at, sources, meta, root, diag_inv):
    count = len(places)
    piece = jax.ShapeDtypeStruct((count, 2, PART + 2 * DIAG, B), jnp.bfloat16)
    return pl.pallas_call(
        lambda *refs: column_body(places, own_at, *refs),
        out_shape=[piece] * 4,
        in_specs=[
            pl.BlockSpec(memory_space=pltpu.SMEM),
            pl.BlockSpec(memory_space=pl.ANY),
            pl.BlockSpec(memory_space=pltpu.VMEM),
        ]
        + [pl.BlockSpec(memory_space=pl.ANY)] * len(sources),
        out_specs=[pl.BlockSpec(memory_space=pltpu.VMEM)] * 4,
        scratch_shapes=[
            pltpu.VMEM((count, ROWS, 2 * M * B), jnp.bfloat16),
            pltpu.VMEM((count, 4, 2, 2 * B, B), jnp.bfloat16),
            pltpu.VMEM((ROWS, 2 * B), jnp.bfloat16),
            pltpu.VMEM((B, 2 * B), jnp.float32),
            pltpu.SemaphoreType.DMA((count,)),
            pltpu.SemaphoreType.DMA((count,)),
        ],
        compiler_params=pltpu.CompilerParams(vmem_limit_bytes=40 * 2**20),
        cost_estimate=pl.CostEstimate(
            flops=2 * count * ROWS * 2 * M * B * 2 * B,
            bytes_accessed=count * (2 * ROWS * 2 * M * B),
            transcendentals=0,
        ),
        name="columns",
    )(meta, root, diag_inv, *sources)


def weighted(coef, which, mine, other):
    own_real, own_imag = mine[0].astype(jnp.float32), mine[1].astype(jnp.float32)
    far_real, far_imag = other[0].astype(jnp.float32), other[1].astype(jnp.float32)
    value = (
        coef[0, 2 * which] * own_imag
        + coef[0, 2 * which + 1] * own_real
        + coef[1, 2 * which] * far_imag
        + coef[1, 2 * which + 1] * far_real
    )
    return value[:PART], value[PART : PART + DIAG] + value[PART + DIAG :]


def pair_body(coef, mine, other, out):
    for j in range(out.shape[0]):
        for which in range(2):
            rows, diag = weighted(coef, which, mine[j], other[j])
            out[j, which, :PART, :] = rows.astype(jnp.bfloat16)
            out[j, which, PART:, :] = diag.astype(jnp.bfloat16)


def pair_sums(coef, mine, other):
    count = mine.shape[0]
    return pl.pallas_call(
        pair_body,
        out_shape=jax.ShapeDtypeStruct((count, 2, PART + DIAG, B), jnp.bfloat16),
        in_specs=[pl.BlockSpec(memory_space=pltpu.SMEM)]
        + [pl.BlockSpec(memory_space=pltpu.VMEM)] * 2,
        out_specs=pl.BlockSpec(memory_space=pltpu.VMEM),
        cost_estimate=pl.CostEstimate(flops=0, bytes_accessed=6 * 2**20, transcendentals=0),
        name="pair_sums",
    )(coef, mine, other)


def four_body(coef, mine, other, far, *outs):
    for j, out in enumerate(outs):
        for which in range(2):
            rows, diag = weighted(coef, which, mine[j], other[j])
            rows = rows + far[j, which, :PART, :].astype(jnp.float32)
            diag = diag + far[j, which, PART:, :].astype(jnp.float32)
            out[which, :PART, :] = rows.astype(jnp.bfloat16)
            out[which, PART:, :] = diag.astype(jnp.bfloat16)


def four_sums(coef, mine, other, far):
    count = mine.shape[0]
    return pl.pallas_call(
        four_body,
        out_shape=[jax.ShapeDtypeStruct((2, PART + DIAG, B), jnp.bfloat16)] * count,
        in_specs=[pl.BlockSpec(memory_space=pltpu.SMEM)]
        + [pl.BlockSpec(memory_space=pltpu.VMEM)] * 3,
        out_specs=[pl.BlockSpec(memory_space=pltpu.VMEM)] * count,
        cost_estimate=pl.CostEstimate(flops=0, bytes_accessed=6 * 2**20, transcendentals=0),
        name="four_sums",
    )(coef, mine, other, far)


def place_body(owners, *refs):
    pieces, (rows_out, diag_out) = refs[:-2], refs[-2:]
    total = jnp.zeros(diag_out.shape, jnp.float32)
    for n, piece in enumerate(pieces):
        owner = owners[n]
        for which in range(2):
            rows_out[which, owner] = piece[which, :PART, :].astype(jnp.float32)
        total = total + piece[:, PART:, :].astype(jnp.float32)
    diag_out[...] = total


def placed(owners, pieces):
    return pl.pallas_call(
        place_body,
        out_shape=[
            jax.ShapeDtypeStruct((2, NODES, PART, B), jnp.float32),
            jax.ShapeDtypeStruct((2, DIAG, B), jnp.float32),
        ],
        in_specs=[pl.BlockSpec(memory_space=pltpu.SMEM)]
        + [pl.BlockSpec(memory_space=pltpu.VMEM)] * len(pieces),
        out_specs=[pl.BlockSpec(memory_space=pltpu.VMEM)] * 2,
        compiler_params=pltpu.CompilerParams(vmem_limit_bytes=24 * 2**20),
        name="placed",
    )(owners, *pieces)


def on_device(root_inverse, factor_columns, diagonal_inverse, pattern, pole_weights, pole_shifts):
    node = lax.axis_index("snode")
    pole = lax.axis_index("pole")
    x, z, y = node // (SZ * SY), (node // SY) % SZ, node % SY
    weight_real, weight_imag = pole_weights[0, 0], pole_weights[0, 1]
    shift_real, shift_imag = pole_shifts[0, 0], pole_shifts[0, 1]
    own_coef = jnp.stack(
        [
            weight_real,
            weight_imag,
            weight_real * shift_real - weight_imag * shift_imag,
            weight_real * shift_imag + weight_imag * shift_real,
        ]
    )[None]
    coef = jnp.concatenate([own_coef, lax.ppermute(own_coef, "pole", CORE)])
    own = factor_columns[0, 0]
    factors = (own, send(own, dz=1))
    pieces, owners = [], []
    for dz in range(2):
        left, right = gathered(factors[dz])
        for places_of in (INNER, OUTER):
            sources, slots, places = [], {}, []

            def source(key, array):
                if key not in slots:
                    slots[key] = len(sources)
                    sources.append(array)
                return slots[key]

            for dx, dy in places_of:
                places.append(
                    [(source(("l", dy, h), left[dy][h]), RING.index(dx)) for h in range(2)]
                    + [(source(("r", dx, h), right[dx][h]), RING.index(dy)) for h in range(2)]
                )
            nodes = jnp.stack(
                [
                    ((x + dx) % SX * SZ + (z + dz) % SZ) * SY + (y + dy) % SY
                    for dx, dy in places_of
                ]
            )
            meta = jnp.concatenate(
                [
                    jnp.take(pattern, nodes, axis=0).reshape(-1),
                    jnp.stack([node * (ROWS // B), pole]).astype(jnp.int32),
                ]
            )
            own_at = 0 if dz == 0 and places_of is INNER else None
            keep_near, keep_far, give_near, give_far = columns_of(
                places, own_at, sources, meta, root_inverse, diagonal_inverse[0, 0]
            )
            got_far = lax.ppermute(give_far, "pole", CORE)
            got_near = lax.ppermute(give_near, "pole", CORE)
            far = lax.ppermute(pair_sums(coef, keep_far, got_far), "pole", Z_HI)
            sums = four_sums(coef, keep_near, got_near, far)
            for (dx, dy), value in zip(places_of, sums):
                moved = (dx, dz, dy) != (0, 0, 0)
                pieces.append(send(value, dx=dx, dz=dz, dy=dy) if moved else value)
                owners.append(((x - dx) % SX * SZ + (z - dz) % SZ) * SY + (y - dy) % SY)
    rows_out, diag_out = placed(jnp.stack(owners).astype(jnp.int32), pieces)
    return rows_out[:, None], diag_out[:, None]


def solution(mesh):
    in_specs = (
        P("pole", None, None, "snode", None),
        P("pole", "snode", None, None, None),
        P("pole", "snode", None, None, None),
        P(),
        P("pole", None),
        P("pole", None),
    )
    out_specs = (P(None, "snode", None, "pole", None), P(None, "snode", "pole", None))
    return jax.shard_map(
        on_device, mesh=mesh, in_specs=in_specs, out_specs=out_specs, check_vma=False
    )
```

```python
import jax
import jax.numpy as jnp
from jax import lax
from jax.experimental import pallas as pl
from jax.experimental.pallas import tpu as pltpu
from jax.sharding import PartitionSpec as P

B = 128
M = 8
ROWS = 384
PART = 96
DIAG = 32
SX, SZ, SY = 4, 2, 4
COST = pl.CostEstimate(flops=0, bytes_accessed=1, transcendentals=0)
AHEAD = 4
RING = (0, 1, -1, 2)
CORE = [(p, p ^ 1) for p in range(4)]
Z_HI = [(p, p ^ 2) for p in range(4)]
PLANES = [[(x * SZ + z) * SY + y for x in range(SX) for y in range(SY)] for z in range(SZ)]
ALL = [(a, b) for a in range(4) for b in range(4)]
INNER = [(a, b) for a in range(3) for b in range(3)]
OUTER = [(a, 3) for a in range(4)] + [(3, b) for b in range(3)]


def shift(dx=0, dz=0, dy=0):
    return [
        (
            (x * SZ + z) * SY + y,
            (((x + dx) % SX) * SZ + (z + dz) % SZ) * SY + (y + dy) % SY,
        )
        for x in range(SX)
        for z in range(SZ)
        for y in range(SY)
    ]


def across():
    nodes = SX * SZ * SY
    return [
        (p * nodes + a, (p ^ 2) * nodes + b) for p in range(4) for a, b in shift(dz=1)
    ]


def send(value, **by):
    return lax.ppermute(value, "snode", shift(**by))


def copies_body(plan, n_in, n_out, *refs):
    ins, outs = refs[:n_in], refs[n_in : n_in + n_out]
    stages, sems = refs[n_in + n_out : -1], refs[-1]
    first, second = [], []
    for n, (source, targets) in enumerate(plan):
        first.append(pltpu.make_async_copy(source(ins), stages[n], sems.at[n]))
        first[-1].start()
    for n, (source, targets) in enumerate(plan):
        first[n].wait()
        for target in targets:
            at = len(plan) + len(second)
            second.append(pltpu.make_async_copy(stages[n], target(outs), sems.at[at]))
            second[-1].start()
    for copy in second:
        copy.wait()


def copied(name, plan, piece, arrays, shapes):
    n_copies = len(plan) + sum(len(targets) for _, targets in plan)
    return pl.pallas_call(
        lambda *refs: copies_body(plan, len(arrays), len(shapes), *refs),
        out_shape=[jax.ShapeDtypeStruct(shape, jnp.bfloat16) for shape in shapes],
        in_specs=[pl.BlockSpec(memory_space=pl.ANY)] * len(arrays),
        out_specs=[pl.BlockSpec(memory_space=pltpu.HBM)] * len(shapes),
        scratch_shapes=[pltpu.VMEM(piece, jnp.bfloat16)] * len(plan)
        + [pltpu.SemaphoreType.DMA((n_copies,))],
        compiler_params=pltpu.CompilerParams(vmem_limit_bytes=8 * 2**20),
        cost_estimate=COST,
        name=name,
    )(*arrays)


CROSS = (2, 4, 2, 2 * B, B)


def own_rings(factor):
    parts = factor.reshape(2, 2, 2, 2 * B, B).transpose(1, 2, 0, 3, 4)
    arrays = [parts[0]] + [send(parts[0], dx=-d) for d in RING[1:]]
    arrays += [parts[1]] + [send(parts[1], dy=-d) for d in RING[1:]]
    plan = []
    for n in range(8):
        side, at = n // 4, n % 4
        targets = [
            lambda outs, s=side, at=at: outs[s].at[:, at],
            lambda outs, s=side, at=at: outs[2].at[s, :, at],
        ]
        plan.append((lambda ins, n=n: ins[n], targets))
    return copied("own_rings", plan, CROSS[:1] + CROSS[2:], arrays, [CROSS, CROSS, (2,) + CROSS])


def crossed(left, right):
    found = [
        (send(left, dy=-1), send(left, dy=1)),
        (send(right, dx=-1), send(right, dx=1)),
    ]
    arrays = [*found[0], *found[1]]
    plan = [
        (lambda ins, n=n: ins[n].at[1 - n % 2], [lambda outs, n=n: outs[n]]) for n in range(4)
    ]
    halves = copied("halves", plan, CROSS[1:], arrays, [CROSS[1:]] * 4)
    far = [
        (send(halves[1], dy=1), send(halves[0], dy=-1)),
        (send(halves[3], dx=1), send(halves[2], dx=-1)),
    ]
    return [left, *found[0], *far[0]], [right, *found[1], *far[1]]


def factor_copies(places, left, right, factors):
    dys = sorted({a for a, _ in places})
    dxs = sorted({b for _, b in places})
    found = []
    for side, ours, others in ((1, dxs, dys), (0, dys, dxs)):
        sources = (left, right)[side]
        for one in ours:
            far = [o for o in others if ((o, one) if side else (one, o)) in places]
            span = pl.ds(far[0], len(far))
            for h in range(2):
                ref = sources[one].at[h, span] if one < 3 else sources[3 + h].at[span]
                if side:
                    found.append((ref, factors.at[span, one, 2 + h]))
                else:
                    found.append((ref, factors.at[one, span, h]))
    return found


def column_body(places, with_own, meta, root, diag_inv, *refs):
    count = len(places)
    left, right = refs[:5], refs[5:10]
    keep, give, blocks, factors, column, total, root_sems, sems = refs[-8:]

    def fetch(j, i):
        slot = j % AHEAD
        for h in range(2):
            pltpu.make_async_copy(
                root.at[0, h, meta[j * M + i]],
                blocks.at[slot, i, :, pl.ds(h * B, B)],
                root_sems.at[slot],
            ).start()

    copies = [
        pltpu.make_async_copy(source, target, sems.at[n])
        for n, (source, target) in enumerate(factor_copies(places, left, right, factors))
    ]
    for copy in copies:
        copy.start()

    @pl.loop(0, (AHEAD - 1) * M)
    def _(n):
        fetch(n // M, n % M)

    for copy in copies:
        copy.wait()
    first_block = meta[count * M]
    pole = meta[count * M + 1]

    @pl.loop(0, count)
    def _(j):
        @pl.when(j + AHEAD - 1 < count)
        def _():
            for i in range(M):
                fetch(j + AHEAD - 1, i)

        dy = meta[count * M + 2 + 2 * j]
        dx = meta[count * M + 3 + 2 * j]
        slot = j % AHEAD

        pltpu.make_async_copy(blocks.at[slot], blocks.at[slot], root_sems.at[slot]).wait()

        product = None
        for i in range(M):
            at = pl.ds((i % 2) * B, B)
            real, imag = factors[dy, dx, i // 2, 0, at, :], factors[dy, dx, i // 2, 1, at, :]
            weights = jnp.concatenate(
                [
                    jnp.concatenate([real, imag], axis=1),
                    jnp.concatenate([-imag, real], axis=1),
                ],
                axis=0,
            )
            term = jnp.dot(blocks[slot, i], weights, preferred_element_type=jnp.float32)
            product = term if product is None else product + term
        column[...] = (-product).astype(jnp.bfloat16)
        total[...] = jnp.zeros_like(total)

        @pl.loop(0, M)
        def _(i):
            local = meta[j * M + i] - first_block

            @pl.when((local >= 0) & (local < ROWS // B))
            def _():
                rows = column[pl.ds(pl.multiple_of(local * B, B), B), :]
                real, imag = rows[:, :B], rows[:, B:]
                values = jnp.concatenate(
                    [
                        jnp.concatenate([real, imag], axis=1),
                        jnp.concatenate([-imag, real], axis=1),
                    ],
                    axis=0,
                )
                at = pl.ds(pl.multiple_of((i % 2) * B, B), B)
                factor = jnp.concatenate(
                    [factors[dy, dx, i // 2, 0, at, :], factors[dy, dx, i // 2, 1, at, :]], axis=0
                )
                total[...] += lax.dot_general(
                    factor, values, (((0,), (0,)), ((), ())), preferred_element_type=jnp.float32
                )

        if with_own:

            @pl.when(j == 0)
            def _():
                total[:, :B] -= diag_inv[0].astype(jnp.float32)
                total[:, B:] -= diag_inv[1].astype(jnp.float32)

        for n in range(4):
            out, e = (keep, give)[n >> 1], n & 1
            part = pole ^ ((e << 1) | (n >> 1))
            rows_at = pl.multiple_of(part * PART, PART)
            diag_at = pl.multiple_of(part * DIAG, DIAG)
            for h in range(2):
                lanes = slice(h * B, (h + 1) * B)
                out[e, j, h, :PART, :] = column[pl.ds(rows_at, PART), lanes]
                share = -total[pl.ds(diag_at, DIAG), lanes]
                coarse = share.astype(jnp.bfloat16)
                out[e, j, h, PART : PART + DIAG, :] = coarse
                rest = share - coarse.astype(jnp.float32)
                out[e, j, h, PART + DIAG :, :] = rest.astype(jnp.bfloat16)


def columns_of(places, with_own, left, right, meta, root, diag_inv, after):
    count = len(places)
    piece = jax.ShapeDtypeStruct((2, count, 2, PART + 2 * DIAG, B), jnp.bfloat16)
    n_copies = 2 * (len({a for a, _ in places}) + len({b for _, b in places}))
    return pl.pallas_call(
        lambda *refs: column_body(places, with_own, *refs),
        out_shape=[piece] * 2,
        in_specs=[
            pl.BlockSpec(memory_space=pltpu.SMEM),
            pl.BlockSpec(memory_space=pl.ANY),
            pl.BlockSpec(memory_space=pltpu.VMEM),
        ]
        + [pl.BlockSpec(memory_space=pl.ANY)] * (10 + len(after)),
        out_specs=[pl.BlockSpec(memory_space=pltpu.VMEM)] * 2,
        scratch_shapes=[
            pltpu.VMEM((AHEAD, M, ROWS, 2 * B), jnp.bfloat16),
            pltpu.VMEM((4, 4, 4, 2, 2 * B, B), jnp.bfloat16),
            pltpu.VMEM((ROWS, 2 * B), jnp.bfloat16),
            pltpu.VMEM((B, 2 * B), jnp.float32),
            pltpu.SemaphoreType.DMA((AHEAD,)),
            pltpu.SemaphoreType.DMA((n_copies,)),
        ],
        compiler_params=pltpu.CompilerParams(vmem_limit_bytes=60 * 2**20),
        cost_estimate=pl.CostEstimate(
            flops=2 * count * ROWS * 2 * M * B * 2 * B,
            bytes_accessed=count * (2 * M * B * B * 2 + 2 * M * ROWS * B * 2),
            transcendentals=0,
        ),
        name="columns",
    )(meta, root, diag_inv, *left, *right, *after)


def weighted(coef, which, mine, other):
    own_real, own_imag = mine[0].astype(jnp.float32), mine[1].astype(jnp.float32)
    far_real, far_imag = other[0].astype(jnp.float32), other[1].astype(jnp.float32)
    value = (
        coef[0, 2 * which] * own_imag
        + coef[0, 2 * which + 1] * own_real
        + coef[1, 2 * which] * far_imag
        + coef[1, 2 * which + 1] * far_real
    )
    return value[:PART], value[PART : PART + DIAG] + value[PART + DIAG :]


def pair_body(parts, coef, mine, other, *refs):
    outs = refs[-len(parts) :]

    @pl.loop(0, mine.shape[1])
    def _(j):
        for e, out in zip(parts, outs):
            for which in range(2):
                rows, diag = weighted(coef, which, mine[e, j], other[e, j])
                out[j, which, :PART, :] = rows.astype(jnp.bfloat16)
                out[j, which, PART:, :] = diag.astype(jnp.bfloat16)


def pair_sums(parts, coef, mine, other, after):
    count = mine.shape[1]
    return pl.pallas_call(
        lambda *refs: pair_body(parts, *refs),
        out_shape=[jax.ShapeDtypeStruct((count, 2, PART + DIAG, B), jnp.bfloat16)] * len(parts),
        in_specs=[pl.BlockSpec(memory_space=pltpu.SMEM)]
        + [pl.BlockSpec(memory_space=pltpu.VMEM)] * 2
        + [pl.BlockSpec(memory_space=pl.ANY)] * len(after),
        out_specs=[pl.BlockSpec(memory_space=pltpu.VMEM)] * len(parts),
        compiler_params=pltpu.CompilerParams(vmem_limit_bytes=16 * 2**20),
        cost_estimate=COST,
        name="pair_sums",
    )(coef, mine, other, *after)


def own_body(coef, order, mine, other, far, out):
    @pl.loop(0, far.shape[0])
    def _(j):
        at = order[j]
        for which in range(2):
            rows, diag = weighted(coef, which, mine[0, j], other[0, j])
            rows = rows + far[j, which, :PART, :].astype(jnp.float32)
            diag = diag + far[j, which, PART:, :].astype(jnp.float32)
            out[at, which, :PART, :] = rows.astype(jnp.bfloat16)
            out[at, which, PART:, :] = diag.astype(jnp.bfloat16)


def own_sums(coef, order, mine, other, far):
    return pl.pallas_call(
        own_body,
        out_shape=jax.ShapeDtypeStruct(far.shape, jnp.bfloat16),
        in_specs=[pl.BlockSpec(memory_space=pltpu.SMEM)] * 2
        + [pl.BlockSpec(memory_space=pltpu.VMEM)] * 3,
        out_specs=pl.BlockSpec(memory_space=pltpu.VMEM),
        compiler_params=pltpu.CompilerParams(vmem_limit_bytes=16 * 2**20),
        cost_estimate=COST,
        name="own_sums",
    )(coef, order, mine, other, far)


def next_body(order, *refs):
    out, start = refs[-1], 0
    for near, far in zip(refs[:-1:2], refs[1:-1:2]):

        @pl.loop(0, near.shape[0])
        def _(j, start=start, near=near, far=far):
            value = near[j].astype(jnp.float32) + far[j].astype(jnp.float32)
            out[order[start + j]] = value.astype(jnp.bfloat16)

        start += near.shape[0]


def next_sums(order, pairs):
    return pl.pallas_call(
        next_body,
        out_shape=jax.ShapeDtypeStruct((SX * SY, 2, PART + DIAG, B), jnp.bfloat16),
        in_specs=[pl.BlockSpec(memory_space=pltpu.SMEM)]
        + [pl.BlockSpec(memory_space=pltpu.VMEM)] * (2 * len(pairs)),
        out_specs=pl.BlockSpec(memory_space=pltpu.VMEM),
        compiler_params=pltpu.CompilerParams(vmem_limit_bytes=16 * 2**20),
        cost_estimate=COST,
        name="next_sums",
    )(order, *[piece for pair in pairs for piece in pair])


def place_body(plane, own, other, rows_out, diag_out):
    diag_out[...] = jnp.zeros_like(diag_out)
    for n, pieces in enumerate((own, other)):
        z = plane[n]

        @pl.loop(0, SX * SY)
        def _(j, pieces=pieces, z=z):
            owner = (j // SY * SZ + z) * SY + j % SY
            for which in range(2):
                rows_out[which, owner] = pieces[j, which, :PART, :].astype(jnp.float32)
            diag_out[...] += pieces[j, :, PART:, :].astype(jnp.float32)


def placed(plane, own, other):
    return pl.pallas_call(
        place_body,
        out_shape=[
            jax.ShapeDtypeStruct((2, SX * SZ * SY, PART, B), jnp.float32),
            jax.ShapeDtypeStruct((2, DIAG, B), jnp.float32),
        ],
        in_specs=[pl.BlockSpec(memory_space=pltpu.SMEM)]
        + [pl.BlockSpec(memory_space=pltpu.VMEM)] * 2,
        out_specs=[pl.BlockSpec(memory_space=pltpu.VMEM)] * 2,
        compiler_params=pltpu.CompilerParams(vmem_limit_bytes=16 * 2**20),
        name="placed",
    )(plane, own, other)


def in_plane(value):
    return lax.all_to_all(
        value, "snode", split_axis=0, concat_axis=0, axis_index_groups=PLANES, tiled=True
    )


def on_device(root_inverse, factor_columns, diagonal_inverse, pattern, pole_weights, pole_shifts):
    node = lax.axis_index("snode")
    pole = lax.axis_index("pole")
    x, z, y = node // (SZ * SY), (node // SY) % SZ, node % SY
    weight_real, weight_imag = pole_weights[0, 0], pole_weights[0, 1]
    shift_real, shift_imag = pole_shifts[0, 0], pole_shifts[0, 1]
    own_coef = jnp.stack(
        [
            weight_real,
            weight_imag,
            weight_real * shift_real - weight_imag * shift_imag,
            weight_real * shift_imag + weight_imag * shift_real,
        ]
    )[None]
    coef = jnp.concatenate([own_coef, lax.ppermute(own_coef, "pole", CORE)])
    left, right, both = own_rings(factor_columns[0, 0])
    both = send(both, dz=1)
    left, right = crossed(left, right)
    plan = [(lambda ins, n=n: ins[0].at[n], [lambda outs, n=n: outs[n]]) for n in range(2)]
    next_left, next_right = copied("next_rings", plan, CROSS, [both], [CROSS, CROSS])

    def chunk(dz, places, left, right, after):
        at = [(RING[a], RING[b]) for a, b in places]
        nodes = jnp.stack(
            [((x + dx) % SX * SZ + (z + dz) % SZ) * SY + (y + dy) % SY for dy, dx in at]
        )
        order = jnp.stack([(x + dx) % SX * SY + (y + dy) % SY for dy, dx in at])
        meta = jnp.concatenate(
            [
                pattern[nodes].reshape(-1),
                jnp.stack([node * (ROWS // B), pole]),
                jnp.array(places, jnp.int32).reshape(-1),
            ]
        ).astype(jnp.int32)
        keep, give = columns_of(
            places, dz == 0, left, right, meta, root_inverse, diagonal_inverse[0, 0], after
        )
        return keep, lax.ppermute(give, "pole", CORE), order.astype(jnp.int32)

    keep, got, order = chunk(0, ALL, left, right, (next_left,))
    (away,) = pair_sums((1,), coef, keep, got, ())
    sums = own_sums(coef, order, keep, got, lax.ppermute(away, "pole", Z_HI))
    own = in_plane(sums)
    left, right = crossed(next_left, next_right)
    keep, got, inner = chunk(1, INNER, left, right, (away,))
    near, away = pair_sums((0, 1), coef, keep, got, ())
    keep, got, outer = chunk(1, OUTER, left, right, (away,))
    pairs = [(near, away), pair_sums((0, 1), coef, keep, got, (sums,))]
    pairs = [
        (send(near, dz=1), lax.ppermute(away, ("pole", "snode"), across()))
        for near, away in pairs
    ]
    other = in_plane(next_sums(jnp.concatenate([inner, outer]), pairs))
    rows_out, diag_out = placed(jnp.stack([z, 1 - z]).astype(jnp.int32), own, other)
    return rows_out[:, None], diag_out[:, None]


def solution(mesh):
    in_specs = (
        P("pole", None, None, "snode", None),
        P("pole", "snode", None, None, None),
        P("pole", "snode", None, None, None),
        P(),
        P("pole", None),
        P("pole", None),
    )
    out_specs = (P(None, "snode", None, "pole", None), P(None, "snode", "pole", None))
    return jax.shard_map(
        on_device, mesh=mesh, in_specs=in_specs, out_specs=out_specs, check_vma=False
    )
```

```python
import jax
import jax.numpy as jnp
from jax import lax
from jax.experimental import pallas as pl
from jax.experimental.pallas import tpu as pltpu
from jax.sharding import PartitionSpec as P

B = 128
M = 8
ROWS = 384
PART = 96
DIAG = 32
SX, SZ, SY = 4, 2, 4
COST = pl.CostEstimate(flops=0, bytes_accessed=1, transcendentals=0)
AHEAD = 4
RING = (0, 1, -1, 2)
CORE = [(p, p ^ 1) for p in range(4)]
Z_HI = [(p, p ^ 2) for p in range(4)]
PLANES = [[(x * SZ + z) * SY + y for x in range(SX) for y in range(SY)] for z in range(SZ)]
ALL = [(a, b) for a in range(4) for b in range(4)]
INNER = [(a, b) for a in range(3) for b in range(3)]
OUTER = [(a, 3) for a in range(4)] + [(3, b) for b in range(3)]


def shift(dx=0, dz=0, dy=0):
    return [
        (
            (x * SZ + z) * SY + y,
            (((x + dx) % SX) * SZ + (z + dz) % SZ) * SY + (y + dy) % SY,
        )
        for x in range(SX)
        for z in range(SZ)
        for y in range(SY)
    ]


def across():
    nodes = SX * SZ * SY
    return [
        (p * nodes + a, (p ^ 2) * nodes + b) for p in range(4) for a, b in shift(dz=1)
    ]


def send(value, **by):
    return lax.ppermute(value, "snode", shift(**by))


def ordered(value, *after):
    return pl.pallas_call(
        lambda *refs: None,
        out_shape=jax.ShapeDtypeStruct(value.shape, value.dtype),
        in_specs=[pl.BlockSpec(memory_space=pl.ANY)] * (1 + len(after)),
        out_specs=pl.BlockSpec(memory_space=pl.ANY),
        input_output_aliases={0: 0},
        compiler_params=pltpu.CompilerParams(vmem_limit_bytes=2**20),
        cost_estimate=COST,
        name="ordered",
    )(value, *after)


def copies_body(plan, n_in, n_out, *refs):
    ins, outs = refs[:n_in], refs[n_in : n_in + n_out]
    stages, sems = refs[n_in + n_out : -1], refs[-1]
    first, second = [], []
    for n, (source, targets) in enumerate(plan):
        first.append(pltpu.make_async_copy(source(ins), stages[n], sems.at[n]))
        first[-1].start()
    for n, (source, targets) in enumerate(plan):
        first[n].wait()
        for target in targets:
            at = len(plan) + len(second)
            second.append(pltpu.make_async_copy(stages[n], target(outs), sems.at[at]))
            second[-1].start()
    for copy in second:
        copy.wait()


def copied(name, plan, piece, arrays, shapes):
    n_copies = len(plan) + sum(len(targets) for _, targets in plan)
    return pl.pallas_call(
        lambda *refs: copies_body(plan, len(arrays), len(shapes), *refs),
        out_shape=[jax.ShapeDtypeStruct(shape, jnp.bfloat16) for shape in shapes],
        in_specs=[pl.BlockSpec(memory_space=pl.ANY)] * len(arrays),
        out_specs=[pl.BlockSpec(memory_space=pltpu.HBM)] * len(shapes),
        scratch_shapes=[pltpu.VMEM(piece, jnp.bfloat16)] * len(plan)
        + [pltpu.SemaphoreType.DMA((n_copies,))],
        compiler_params=pltpu.CompilerParams(vmem_limit_bytes=8 * 2**20),
        cost_estimate=COST,
        name=name,
    )(*arrays)


CROSS = (2, 4, 2, 2 * B, B)


def own_rings(factor):
    parts = factor.reshape(2, 2, 2, 2 * B, B).transpose(1, 2, 0, 3, 4)
    arrays = [parts[0]] + [send(parts[0], dx=-d) for d in RING[1:]]
    arrays += [parts[1]] + [send(parts[1], dy=-d) for d in RING[1:]]
    plan = []
    for n in range(8):
        side, at = n // 4, n % 4
        targets = [
            lambda outs, s=side, at=at: outs[s].at[:, at],
            lambda outs, s=side, at=at: outs[2].at[s, :, at],
        ]
        plan.append((lambda ins, n=n: ins[n], targets))
    return copied("own_rings", plan, CROSS[:1] + CROSS[2:], arrays, [CROSS, CROSS, (2,) + CROSS])


def crossed(left, right):
    found = [
        (send(left, dy=-1), send(left, dy=1)),
        (send(right, dx=-1), send(right, dx=1)),
    ]
    arrays = [*found[0], *found[1]]
    plan = [
        (lambda ins, n=n: ins[n].at[1 - n % 2], [lambda outs, n=n: outs[n]]) for n in range(4)
    ]
    halves = copied("halves", plan, CROSS[1:], arrays, [CROSS[1:]] * 4)
    far = [
        (send(halves[1], dy=1), send(halves[0], dy=-1)),
        (send(halves[3], dx=1), send(halves[2], dx=-1)),
    ]
    return [left, *found[0], *far[0]], [right, *found[1], *far[1]], halves


def factor_copies(places, left, right, factors):
    dys = sorted({a for a, _ in places})
    dxs = sorted({b for _, b in places})
    found = []
    for side, ours, others in ((1, dxs, dys), (0, dys, dxs)):
        sources = (left, right)[side]
        for one in ours:
            far = [o for o in others if ((o, one) if side else (one, o)) in places]
            span = pl.ds(far[0], len(far))
            for h in range(2):
                ref = sources[one].at[h, span] if one < 3 else sources[3 + h].at[span]
                if side:
                    found.append((ref, factors.at[span, one, 2 + h]))
                else:
                    found.append((ref, factors.at[one, span, h]))
    return found


def column_body(places, with_own, meta, root, diag_inv, *refs):
    count = len(places)
    n_side = 3 if places is INNER else 5
    left, right = refs[:n_side], refs[n_side : 2 * n_side]
    keep, give, blocks, factors, column, total, root_sems, sems = refs[-8:]

    def fetch(j, i):
        slot = j % AHEAD
        for h in range(2):
            pltpu.make_async_copy(
                root.at[0, h, meta[j * M + i]],
                blocks.at[slot, i, :, pl.ds(h * B, B)],
                root_sems.at[slot],
            ).start()

    copies = [
        pltpu.make_async_copy(source, target, sems.at[n])
        for n, (source, target) in enumerate(factor_copies(places, left, right, factors))
    ]
    for copy in copies:
        copy.start()

    @pl.loop(0, (AHEAD - 1) * M)
    def _(n):
        fetch(n // M, n % M)

    for copy in copies:
        copy.wait()
    first_block = meta[count * M]
    pole = meta[count * M + 1]

    @pl.loop(0, count)
    def _(j):
        @pl.when(j + AHEAD - 1 < count)
        def _():
            for i in range(M):
                fetch(j + AHEAD - 1, i)

        dy = meta[count * M + 2 + 2 * j]
        dx = meta[count * M + 3 + 2 * j]
        slot = j % AHEAD

        pltpu.make_async_copy(blocks.at[slot], blocks.at[slot], root_sems.at[slot]).wait()

        product = None
        for i in range(M):
            at = pl.ds((i % 2) * B, B)
            real, imag = factors[dy, dx, i // 2, 0, at, :], factors[dy, dx, i // 2, 1, at, :]
            weights = jnp.concatenate(
                [
                    jnp.concatenate([real, imag], axis=1),
                    jnp.concatenate([-imag, real], axis=1),
                ],
                axis=0,
            )
            term = jnp.dot(blocks[slot, i], weights, preferred_element_type=jnp.float32)
            product = term if product is None else product + term
        column[...] = (-product).astype(jnp.bfloat16)
        total[...] = jnp.zeros_like(total)

        @pl.loop(0, M)
        def _(i):
            local = meta[j * M + i] - first_block

            @pl.when((local >= 0) & (local < ROWS // B))
            def _():
                rows = column[pl.ds(pl.multiple_of(local * B, B), B), :]
                real, imag = rows[:, :B], rows[:, B:]
                values = jnp.concatenate(
                    [
                        jnp.concatenate([real, imag], axis=1),
                        jnp.concatenate([-imag, real], axis=1),
                    ],
                    axis=0,
                )
                at = pl.ds(pl.multiple_of((i % 2) * B, B), B)
                factor = jnp.concatenate(
                    [factors[dy, dx, i // 2, 0, at, :], factors[dy, dx, i // 2, 1, at, :]], axis=0
                )
                total[...] += lax.dot_general(
                    factor, values, (((0,), (0,)), ((), ())), preferred_element_type=jnp.float32
                )

        if with_own:

            @pl.when(j == 0)
            def _():
                total[:, :B] -= diag_inv[0].astype(jnp.float32)
                total[:, B:] -= diag_inv[1].astype(jnp.float32)

        for n in range(4):
            out, e = (keep, give)[n >> 1], n & 1
            part = pole ^ ((e << 1) | (n >> 1))
            rows_at = pl.multiple_of(part * PART, PART)
            diag_at = pl.multiple_of(part * DIAG, DIAG)
            for h in range(2):
                lanes = slice(h * B, (h + 1) * B)
                out[e, j, h, :PART, :] = column[pl.ds(rows_at, PART), lanes]
                share = -total[pl.ds(diag_at, DIAG), lanes]
                coarse = share.astype(jnp.bfloat16)
                out[e, j, h, PART : PART + DIAG, :] = coarse
                rest = share - coarse.astype(jnp.float32)
                out[e, j, h, PART + DIAG :, :] = rest.astype(jnp.bfloat16)


def columns_of(places, with_own, left, right, meta, root, diag_inv, after):
    count = len(places)
    piece = jax.ShapeDtypeStruct((2, count, 2, PART + 2 * DIAG, B), jnp.bfloat16)
    n_copies = 2 * (len({a for a, _ in places}) + len({b for _, b in places}))
    n_side = 3 if places is INNER else 5
    sources = [*left[:n_side], *right[:n_side], *after]
    return pl.pallas_call(
        lambda *refs: column_body(places, with_own, *refs),
        out_shape=[piece] * 2,
        in_specs=[
            pl.BlockSpec(memory_space=pltpu.SMEM),
            pl.BlockSpec(memory_space=pl.ANY),
            pl.BlockSpec(memory_space=pltpu.VMEM),
        ]
        + [pl.BlockSpec(memory_space=pl.ANY)] * len(sources),
        out_specs=[pl.BlockSpec(memory_space=pltpu.VMEM)] * 2,
        scratch_shapes=[
            pltpu.VMEM((AHEAD, M, ROWS, 2 * B), jnp.bfloat16),
            pltpu.VMEM((4, 4, 4, 2, 2 * B, B), jnp.bfloat16),
            pltpu.VMEM((ROWS, 2 * B), jnp.bfloat16),
            pltpu.VMEM((B, 2 * B), jnp.float32),
            pltpu.SemaphoreType.DMA((AHEAD,)),
            pltpu.SemaphoreType.DMA((n_copies,)),
        ],
        compiler_params=pltpu.CompilerParams(vmem_limit_bytes=60 * 2**20),
        cost_estimate=pl.CostEstimate(
            flops=2 * count * ROWS * 2 * M * B * 2 * B,
            bytes_accessed=count * (2 * M * B * B * 2 + 2 * M * ROWS * B * 2),
            transcendentals=0,
        ),
        name="columns",
    )(meta, root, diag_inv, *sources)


def weighted(coef, which, mine, other):
    own_real, own_imag = mine[0].astype(jnp.float32), mine[1].astype(jnp.float32)
    far_real, far_imag = other[0].astype(jnp.float32), other[1].astype(jnp.float32)
    value = (
        coef[0, 2 * which] * own_imag
        + coef[0, 2 * which + 1] * own_real
        + coef[1, 2 * which] * far_imag
        + coef[1, 2 * which + 1] * far_real
    )
    return value[:PART], value[PART : PART + DIAG] + value[PART + DIAG :]


def pair_body(parts, coef, mine, other, *refs):
    outs = refs[-len(parts) :]

    @pl.loop(0, mine.shape[1])
    def _(j):
        for e, out in zip(parts, outs):
            for which in range(2):
                rows, diag = weighted(coef, which, mine[e, j], other[e, j])
                out[j, which, :PART, :] = rows.astype(jnp.bfloat16)
                out[j, which, PART:, :] = diag.astype(jnp.bfloat16)


def pair_sums(parts, coef, mine, other, after):
    count = mine.shape[1]
    return pl.pallas_call(
        lambda *refs: pair_body(parts, *refs),
        out_shape=[jax.ShapeDtypeStruct((count, 2, PART + DIAG, B), jnp.bfloat16)] * len(parts),
        in_specs=[pl.BlockSpec(memory_space=pltpu.SMEM)]
        + [pl.BlockSpec(memory_space=pltpu.VMEM)] * 2
        + [pl.BlockSpec(memory_space=pl.ANY)] * len(after),
        out_specs=[pl.BlockSpec(memory_space=pltpu.VMEM)] * len(parts),
        compiler_params=pltpu.CompilerParams(vmem_limit_bytes=16 * 2**20),
        cost_estimate=COST,
        name="pair_sums",
    )(coef, mine, other, *after)


def own_body(coef, order, mine, other, far, out):
    @pl.loop(0, far.shape[0])
    def _(j):
        at = order[j]
        for which in range(2):
            rows, diag = weighted(coef, which, mine[0, j], other[0, j])
            rows = rows + far[j, which, :PART, :].astype(jnp.float32)
            diag = diag + far[j, which, PART:, :].astype(jnp.float32)
            out[at, which, :PART, :] = rows.astype(jnp.bfloat16)
            out[at, which, PART:, :] = diag.astype(jnp.bfloat16)


def own_sums(coef, order, mine, other, far):
    return pl.pallas_call(
        own_body,
        out_shape=jax.ShapeDtypeStruct(far.shape, jnp.bfloat16),
        in_specs=[pl.BlockSpec(memory_space=pltpu.SMEM)] * 2
        + [pl.BlockSpec(memory_space=pltpu.VMEM)] * 3,
        out_specs=pl.BlockSpec(memory_space=pltpu.VMEM),
        compiler_params=pltpu.CompilerParams(vmem_limit_bytes=16 * 2**20),
        cost_estimate=COST,
        name="own_sums",
    )(coef, order, mine, other, far)


def next_body(order, *refs):
    out, start = refs[-1], 0
    for near, far in zip(refs[:-1:2], refs[1:-1:2]):

        @pl.loop(0, near.shape[0])
        def _(j, start=start, near=near, far=far):
            value = near[j].astype(jnp.float32) + far[j].astype(jnp.float32)
            out[order[start + j]] = value.astype(jnp.bfloat16)

        start += near.shape[0]


def next_sums(order, pairs):
    return pl.pallas_call(
        next_body,
        out_shape=jax.ShapeDtypeStruct((SX * SY, 2, PART + DIAG, B), jnp.bfloat16),
        in_specs=[pl.BlockSpec(memory_space=pltpu.SMEM)]
        + [pl.BlockSpec(memory_space=pltpu.VMEM)] * (2 * len(pairs)),
        out_specs=pl.BlockSpec(memory_space=pltpu.VMEM),
        compiler_params=pltpu.CompilerParams(vmem_limit_bytes=16 * 2**20),
        cost_estimate=COST,
        name="next_sums",
    )(order, *[piece for pair in pairs for piece in pair])


def place_body(plane, own, other, rows_out, diag_out):
    diag_out[...] = jnp.zeros_like(diag_out)
    for n, pieces in enumerate((own, other)):
        z = plane[n]

        @pl.loop(0, SX * SY)
        def _(j, pieces=pieces, z=z):
            owner = (j // SY * SZ + z) * SY + j % SY
            for which in range(2):
                rows_out[which, owner] = pieces[j, which, :PART, :].astype(jnp.float32)
            diag_out[...] += pieces[j, :, PART:, :].astype(jnp.float32)


def placed(plane, own, other):
    return pl.pallas_call(
        place_body,
        out_shape=[
            jax.ShapeDtypeStruct((2, SX * SZ * SY, PART, B), jnp.float32),
            jax.ShapeDtypeStruct((2, DIAG, B), jnp.float32),
        ],
        in_specs=[pl.BlockSpec(memory_space=pltpu.SMEM)]
        + [pl.BlockSpec(memory_space=pltpu.VMEM)] * 2,
        out_specs=[pl.BlockSpec(memory_space=pltpu.VMEM)] * 2,
        compiler_params=pltpu.CompilerParams(vmem_limit_bytes=16 * 2**20),
        name="placed",
    )(plane, own, other)


def in_plane(value):
    return lax.all_to_all(
        value, "snode", split_axis=0, concat_axis=0, axis_index_groups=PLANES, tiled=True
    )


def on_device(root_inverse, factor_columns, diagonal_inverse, pattern, pole_weights, pole_shifts):
    node = lax.axis_index("snode")
    pole = lax.axis_index("pole")
    x, z, y = node // (SZ * SY), (node // SY) % SZ, node % SY
    weight_real, weight_imag = pole_weights[0, 0], pole_weights[0, 1]
    shift_real, shift_imag = pole_shifts[0, 0], pole_shifts[0, 1]
    own_coef = jnp.stack(
        [
            weight_real,
            weight_imag,
            weight_real * shift_real - weight_imag * shift_imag,
            weight_real * shift_imag + weight_imag * shift_real,
        ]
    )[None]
    coef = jnp.concatenate([own_coef, lax.ppermute(own_coef, "pole", CORE)])
    left, right, both = own_rings(factor_columns[0, 0])
    both = send(both, dz=1)
    left, right, _ = crossed(left, right)
    plan = [(lambda ins, n=n: ins[0].at[n], [lambda outs, n=n: outs[n]]) for n in range(2)]
    next_left, next_right = copied("next_rings", plan, CROSS, [both], [CROSS, CROSS])

    def chunk(dz, places, left, right, after):
        at = [(RING[a], RING[b]) for a, b in places]
        nodes = jnp.stack(
            [((x + dx) % SX * SZ + (z + dz) % SZ) * SY + (y + dy) % SY for dy, dx in at]
        )
        order = jnp.stack([(x + dx) % SX * SY + (y + dy) % SY for dy, dx in at])
        meta = jnp.concatenate(
            [
                pattern[nodes].reshape(-1),
                jnp.stack([node * (ROWS // B), pole]),
                jnp.array(places, jnp.int32).reshape(-1),
            ]
        ).astype(jnp.int32)
        keep, give = columns_of(
            places, dz == 0, left, right, meta, root_inverse, diagonal_inverse[0, 0], after
        )
        return keep, give, order.astype(jnp.int32)

    def swapped(give, *after):
        return lax.ppermute(ordered(give, *after), "pole", CORE)

    own_keep, own_give, own_order = chunk(0, ALL, left, right, (next_left,))
    left, right, halves = crossed(next_left, next_right)
    own_got = swapped(own_give, halves[0])
    inner_keep, inner_give, inner = chunk(1, INNER, left, right, ())
    inner_got = swapped(inner_give, left[3], left[4], right[3], right[4])
    (own_away,) = pair_sums((1,), coef, own_keep, own_got, ())
    own_far = lax.ppermute(own_away, "pole", Z_HI)
    outer_keep, outer_give, outer = chunk(1, OUTER, left, right, (own_away,))
    outer_got = swapped(outer_give, inner_got)
    pairs = [
        pair_sums((0, 1), coef, inner_keep, inner_got, (outer_give,)),
        pair_sums((0, 1), coef, outer_keep, outer_got, ()),
    ]
    own = in_plane(own_sums(coef, own_order, own_keep, own_got, ordered(own_far, pairs[1][1])))
    pairs = [
        (send(near, dz=1), lax.ppermute(away, ("pole", "snode"), across()))
        for near, away in pairs
    ]
    other = in_plane(next_sums(jnp.concatenate([inner, outer]), pairs))
    rows_out, diag_out = placed(jnp.stack([z, 1 - z]).astype(jnp.int32), own, other)
    return rows_out[:, None], diag_out[:, None]


def solution(mesh):
    in_specs = (
        P("pole", None, None, "snode", None),
        P("pole", "snode", None, None, None),
        P("pole", "snode", None, None, None),
        P(),
        P("pole", None),
        P("pole", None),
    )
    out_specs = (P(None, "snode", None, "pole", None), P(None, "snode", "pole", None))
    return jax.shard_map(
        on_device, mesh=mesh, in_specs=in_specs, out_specs=out_specs, check_vma=False
    )
```

```python
import jax
import jax.numpy as jnp
from jax import lax
from jax.experimental import pallas as pl
from jax.experimental.pallas import tpu as pltpu
from jax.sharding import PartitionSpec as P

B = 128
M = 8
ROWS = 384
PART = 96
DIAG = 32
SX, SZ, SY = 4, 2, 4
COST = pl.CostEstimate(flops=0, bytes_accessed=1, transcendentals=0)
AHEAD = 4
RING = (0, 1, -1, 2)
CORE = [(p, p ^ 1) for p in range(4)]
Z_HI = [(p, p ^ 2) for p in range(4)]
PLANES = [[(x * SZ + z) * SY + y for x in range(SX) for y in range(SY)] for z in range(SZ)]
ALL = [(a, b) for a in range(4) for b in range(4)]
INNER = [(a, b) for a in range(3) for b in range(3)]
OUTER = [(a, 3) for a in range(4)] + [(3, b) for b in range(3)]


def shift(dx=0, dz=0, dy=0):
    return [
        (
            (x * SZ + z) * SY + y,
            (((x + dx) % SX) * SZ + (z + dz) % SZ) * SY + (y + dy) % SY,
        )
        for x in range(SX)
        for z in range(SZ)
        for y in range(SY)
    ]


def across():
    nodes = SX * SZ * SY
    return [
        (p * nodes + a, (p ^ 2) * nodes + b) for p in range(4) for a, b in shift(dz=1)
    ]


def send(value, **by):
    return lax.ppermute(value, "snode", shift(**by))


def ordered(value, *after):
    return pl.pallas_call(
        lambda *refs: None,
        out_shape=jax.ShapeDtypeStruct(value.shape, value.dtype),
        in_specs=[pl.BlockSpec(memory_space=pl.ANY)] * (1 + len(after)),
        out_specs=pl.BlockSpec(memory_space=pl.ANY),
        input_output_aliases={0: 0},
        compiler_params=pltpu.CompilerParams(vmem_limit_bytes=2**20),
        cost_estimate=COST,
        name="ordered",
    )(value, *after)


def copies_body(plan, n_in, n_out, *refs):
    ins, outs = refs[:n_in], refs[n_in : n_in + n_out]
    stages, sems = refs[n_in + n_out : -1], refs[-1]
    first, second = [], []
    for n, (source, targets) in enumerate(plan):
        first.append(pltpu.make_async_copy(source(ins), stages[n], sems.at[n]))
        first[-1].start()
    for n, (source, targets) in enumerate(plan):
        first[n].wait()
        for target in targets:
            at = len(plan) + len(second)
            second.append(pltpu.make_async_copy(stages[n], target(outs), sems.at[at]))
            second[-1].start()
    for copy in second:
        copy.wait()


def copied(name, plan, piece, arrays, shapes):
    n_copies = len(plan) + sum(len(targets) for _, targets in plan)
    return pl.pallas_call(
        lambda *refs: copies_body(plan, len(arrays), len(shapes), *refs),
        out_shape=[jax.ShapeDtypeStruct(shape, jnp.bfloat16) for shape in shapes],
        in_specs=[pl.BlockSpec(memory_space=pl.ANY)] * len(arrays),
        out_specs=[pl.BlockSpec(memory_space=pltpu.HBM)] * len(shapes),
        scratch_shapes=[pltpu.VMEM(piece, jnp.bfloat16)] * len(plan)
        + [pltpu.SemaphoreType.DMA((n_copies,))],
        compiler_params=pltpu.CompilerParams(vmem_limit_bytes=8 * 2**20),
        cost_estimate=COST,
        name=name,
    )(*arrays)


CROSS = (2, 4, 2, 2 * B, B)


def own_rings(factor):
    parts = factor.reshape(2, 2, 2, 2 * B, B).transpose(1, 2, 0, 3, 4)
    arrays = [parts[0]] + [send(parts[0], dx=-d) for d in RING[1:]]
    arrays += [parts[1]] + [send(parts[1], dy=-d) for d in RING[1:]]
    plan = []
    for n in range(8):
        side, at = n // 4, n % 4
        targets = [
            lambda outs, s=side, at=at: outs[s].at[:, at],
            lambda outs, s=side, at=at: outs[2].at[s, :, at],
        ]
        plan.append((lambda ins, n=n: ins[n], targets))
    return copied("own_rings", plan, CROSS[:1] + CROSS[2:], arrays, [CROSS, CROSS, (2,) + CROSS])


def crossed(left, right):
    found = [
        (send(left, dy=-1), send(left, dy=1)),
        (send(right, dx=-1), send(right, dx=1)),
    ]
    arrays = [*found[0], *found[1]]
    plan = [
        (lambda ins, n=n: ins[n].at[1 - n % 2], [lambda outs, n=n: outs[n]]) for n in range(4)
    ]
    halves = copied("halves", plan, CROSS[1:], arrays, [CROSS[1:]] * 4)
    far = [
        (send(halves[1], dy=1), send(halves[0], dy=-1)),
        (send(halves[3], dx=1), send(halves[2], dx=-1)),
    ]
    return [left, *found[0], *far[0]], [right, *found[1], *far[1]], halves


def factor_copies(places, left, right, factors):
    dys = sorted({a for a, _ in places})
    dxs = sorted({b for _, b in places})
    found = []
    for side, ours, others in ((1, dxs, dys), (0, dys, dxs)):
        sources = (left, right)[side]
        for one in ours:
            far = [o for o in others if ((o, one) if side else (one, o)) in places]
            span = pl.ds(far[0], len(far))
            for h in range(2):
                ref = sources[one].at[h, span] if one < 3 else sources[3 + h].at[span]
                if side:
                    found.append((ref, factors.at[span, one, 2 + h]))
                else:
                    found.append((ref, factors.at[one, span, h]))
    return found


def column_body(places, with_own, meta, root, diag_inv, *refs):
    count = len(places)
    n_side = 3 if places is INNER else 5
    left, right = refs[:n_side], refs[n_side : 2 * n_side]
    keep, give, blocks, factors, column, total, root_sems, sems = refs[-8:]

    def fetch(j, i):
        slot = j % AHEAD
        for h in range(2):
            pltpu.make_async_copy(
                root.at[0, h, meta[j * M + i]],
                blocks.at[slot, i, :, pl.ds(h * B, B)],
                root_sems.at[slot],
            ).start()

    copies = [
        pltpu.make_async_copy(source, target, sems.at[n])
        for n, (source, target) in enumerate(factor_copies(places, left, right, factors))
    ]
    for copy in copies:
        copy.start()

    @pl.loop(0, (AHEAD - 1) * M)
    def _(n):
        fetch(n // M, n % M)

    for copy in copies:
        copy.wait()
    first_block = meta[count * M]
    pole = meta[count * M + 1]

    @pl.loop(0, count)
    def _(j):
        @pl.when(j + AHEAD - 1 < count)
        def _():
            for i in range(M):
                fetch(j + AHEAD - 1, i)

        dy = meta[count * M + 2 + 2 * j]
        dx = meta[count * M + 3 + 2 * j]
        slot = j % AHEAD

        pltpu.make_async_copy(blocks.at[slot], blocks.at[slot], root_sems.at[slot]).wait()

        product = None
        for i in range(M):
            at = pl.ds((i % 2) * B, B)
            real, imag = factors[dy, dx, i // 2, 0, at, :], factors[dy, dx, i // 2, 1, at, :]
            weights = jnp.concatenate(
                [
                    jnp.concatenate([real, imag], axis=1),
                    jnp.concatenate([-imag, real], axis=1),
                ],
                axis=0,
            )
            term = jnp.dot(blocks[slot, i], weights, preferred_element_type=jnp.float32)
            product = term if product is None else product + term
        column[...] = (-product).astype(jnp.bfloat16)
        total[...] = jnp.zeros_like(total)

        @pl.loop(0, M)
        def _(i):
            local = meta[j * M + i] - first_block

            @pl.when((local >= 0) & (local < ROWS // B))
            def _():
                rows = column[pl.ds(pl.multiple_of(local * B, B), B), :]
                real, imag = rows[:, :B], rows[:, B:]
                values = jnp.concatenate(
                    [
                        jnp.concatenate([real, imag], axis=1),
                        jnp.concatenate([-imag, real], axis=1),
                    ],
                    axis=0,
                )
                at = pl.ds(pl.multiple_of((i % 2) * B, B), B)
                factor = jnp.concatenate(
                    [factors[dy, dx, i // 2, 0, at, :], factors[dy, dx, i // 2, 1, at, :]], axis=0
                )
                total[...] += lax.dot_general(
                    factor, values, (((0,), (0,)), ((), ())), preferred_element_type=jnp.float32
                )

        if with_own:

            @pl.when(j == 0)
            def _():
                total[:, :B] -= diag_inv[0].astype(jnp.float32)
                total[:, B:] -= diag_inv[1].astype(jnp.float32)

        for n in range(4):
            out, e = (keep, give)[n >> 1], n & 1
            part = pole ^ ((e << 1) | (n >> 1))
            rows_at = pl.multiple_of(part * PART, PART)
            diag_at = pl.multiple_of(part * DIAG, DIAG)
            for h in range(2):
                lanes = slice(h * B, (h + 1) * B)
                out[e, j, h, :PART, :] = column[pl.ds(rows_at, PART), lanes]
                share = -total[pl.ds(diag_at, DIAG), lanes]
                coarse = share.astype(jnp.bfloat16)
                out[e, j, h, PART : PART + DIAG, :] = coarse
                rest = share - coarse.astype(jnp.float32)
                out[e, j, h, PART + DIAG :, :] = rest.astype(jnp.bfloat16)


def columns_of(places, with_own, left, right, meta, root, diag_inv, after):
    count = len(places)
    piece = jax.ShapeDtypeStruct((2, count, 2, PART + 2 * DIAG, B), jnp.bfloat16)
    n_copies = 2 * (len({a for a, _ in places}) + len({b for _, b in places}))
    n_side = 3 if places is INNER else 5
    sources = [*left[:n_side], *right[:n_side], *after]
    return pl.pallas_call(
        lambda *refs: column_body(places, with_own, *refs),
        out_shape=[piece] * 2,
        in_specs=[
            pl.BlockSpec(memory_space=pltpu.SMEM),
            pl.BlockSpec(memory_space=pl.ANY),
            pl.BlockSpec(memory_space=pltpu.VMEM),
        ]
        + [pl.BlockSpec(memory_space=pl.ANY)] * len(sources),
        out_specs=[pl.BlockSpec(memory_space=pltpu.VMEM)] * 2,
        scratch_shapes=[
            pltpu.VMEM((AHEAD, M, ROWS, 2 * B), jnp.bfloat16),
            pltpu.VMEM((4, 4, 4, 2, 2 * B, B), jnp.bfloat16),
            pltpu.VMEM((ROWS, 2 * B), jnp.bfloat16),
            pltpu.VMEM((B, 2 * B), jnp.float32),
            pltpu.SemaphoreType.DMA((AHEAD,)),
            pltpu.SemaphoreType.DMA((n_copies,)),
        ],
        compiler_params=pltpu.CompilerParams(vmem_limit_bytes=60 * 2**20),
        cost_estimate=pl.CostEstimate(
            flops=2 * count * ROWS * 2 * M * B * 2 * B,
            bytes_accessed=count * (2 * M * B * B * 2 + 2 * M * ROWS * B * 2),
            transcendentals=0,
        ),
        name="columns",
    )(meta, root, diag_inv, *sources)


def weighted(coef, which, mine, other):
    own_real, own_imag = mine[0].astype(jnp.float32), mine[1].astype(jnp.float32)
    far_real, far_imag = other[0].astype(jnp.float32), other[1].astype(jnp.float32)
    value = (
        coef[0, 2 * which] * own_imag
        + coef[0, 2 * which + 1] * own_real
        + coef[1, 2 * which] * far_imag
        + coef[1, 2 * which + 1] * far_real
    )
    return value[:PART], value[PART : PART + DIAG] + value[PART + DIAG :]


def pair_body(parts, coef, mine, other, *refs):
    outs = refs[-len(parts) :]

    @pl.loop(0, mine.shape[1])
    def _(j):
        for e, out in zip(parts, outs):
            for which in range(2):
                rows, diag = weighted(coef, which, mine[e, j], other[e, j])
                out[j, which, :PART, :] = rows.astype(jnp.bfloat16)
                out[j, which, PART:, :] = diag.astype(jnp.bfloat16)


def pair_sums(parts, coef, mine, other, after):
    count = mine.shape[1]
    return pl.pallas_call(
        lambda *refs: pair_body(parts, *refs),
        out_shape=[jax.ShapeDtypeStruct((count, 2, PART + DIAG, B), jnp.bfloat16)] * len(parts),
        in_specs=[pl.BlockSpec(memory_space=pltpu.SMEM)]
        + [pl.BlockSpec(memory_space=pltpu.VMEM)] * 2
        + [pl.BlockSpec(memory_space=pl.ANY)] * len(after),
        out_specs=[pl.BlockSpec(memory_space=pltpu.VMEM)] * len(parts),
        compiler_params=pltpu.CompilerParams(vmem_limit_bytes=16 * 2**20),
        cost_estimate=COST,
        name="pair_sums",
    )(coef, mine, other, *after)


def own_body(coef, order, mine, other, far, out):
    @pl.loop(0, far.shape[0])
    def _(j):
        at = order[j]
        for which in range(2):
            rows, diag = weighted(coef, which, mine[0, j], other[0, j])
            rows = rows + far[j, which, :PART, :].astype(jnp.float32)
            diag = diag + far[j, which, PART:, :].astype(jnp.float32)
            out[at, which, :PART, :] = rows.astype(jnp.bfloat16)
            out[at, which, PART:, :] = diag.astype(jnp.bfloat16)


def own_sums(coef, order, mine, other, far):
    return pl.pallas_call(
        own_body,
        out_shape=jax.ShapeDtypeStruct(far.shape, jnp.bfloat16),
        in_specs=[pl.BlockSpec(memory_space=pltpu.SMEM)] * 2
        + [pl.BlockSpec(memory_space=pltpu.VMEM)] * 3,
        out_specs=pl.BlockSpec(memory_space=pltpu.VMEM),
        compiler_params=pltpu.CompilerParams(vmem_limit_bytes=16 * 2**20),
        cost_estimate=COST,
        name="own_sums",
    )(coef, order, mine, other, far)


def next_body(order, *refs):
    out, start = refs[-1], 0
    for near, far in zip(refs[:-1:2], refs[1:-1:2]):

        @pl.loop(0, near.shape[0])
        def _(j, start=start, near=near, far=far):
            value = near[j].astype(jnp.float32) + far[j].astype(jnp.float32)
            out[order[start + j]] = value.astype(jnp.bfloat16)

        start += near.shape[0]


def next_sums(order, pairs):
    return pl.pallas_call(
        next_body,
        out_shape=jax.ShapeDtypeStruct((SX * SY, 2, PART + DIAG, B), jnp.bfloat16),
        in_specs=[pl.BlockSpec(memory_space=pltpu.SMEM)]
        + [pl.BlockSpec(memory_space=pltpu.VMEM)] * (2 * len(pairs)),
        out_specs=pl.BlockSpec(memory_space=pltpu.VMEM),
        compiler_params=pltpu.CompilerParams(vmem_limit_bytes=16 * 2**20),
        cost_estimate=COST,
        name="next_sums",
    )(order, *[piece for pair in pairs for piece in pair])


def place_body(plane, own, other, rows_out, diag_out):
    diag_out[...] = jnp.zeros_like(diag_out)
    for n, pieces in enumerate((own, other)):
        z = plane[n]

        @pl.loop(0, SX * SY)
        def _(j, pieces=pieces, z=z):
            owner = (j // SY * SZ + z) * SY + j % SY
            for which in range(2):
                rows_out[which, owner] = pieces[j, which, :PART, :].astype(jnp.float32)
            diag_out[...] += pieces[j, :, PART:, :].astype(jnp.float32)


def placed(plane, own, other):
    return pl.pallas_call(
        place_body,
        out_shape=[
            jax.ShapeDtypeStruct((2, SX * SZ * SY, PART, B), jnp.float32),
            jax.ShapeDtypeStruct((2, DIAG, B), jnp.float32),
        ],
        in_specs=[pl.BlockSpec(memory_space=pltpu.SMEM)]
        + [pl.BlockSpec(memory_space=pltpu.VMEM)] * 2,
        out_specs=[pl.BlockSpec(memory_space=pltpu.VMEM)] * 2,
        compiler_params=pltpu.CompilerParams(vmem_limit_bytes=16 * 2**20),
        name="placed",
    )(plane, own, other)


def in_plane(value):
    return lax.all_to_all(
        value, "snode", split_axis=0, concat_axis=0, axis_index_groups=PLANES, tiled=True
    )


def on_device(root_inverse, factor_columns, diagonal_inverse, pattern, pole_weights, pole_shifts):
    node = lax.axis_index("snode")
    pole = lax.axis_index("pole")
    x, z, y = node // (SZ * SY), (node // SY) % SZ, node % SY
    weight_real, weight_imag = pole_weights[0, 0], pole_weights[0, 1]
    shift_real, shift_imag = pole_shifts[0, 0], pole_shifts[0, 1]
    own_coef = jnp.stack(
        [
            weight_real,
            weight_imag,
            weight_real * shift_real - weight_imag * shift_imag,
            weight_real * shift_imag + weight_imag * shift_real,
        ]
    )[None]
    coef = jnp.concatenate([own_coef, lax.ppermute(own_coef, "pole", CORE)])
    left, right, both = own_rings(factor_columns[0, 0])
    both = send(both, dz=1)
    left, right, _ = crossed(left, right)
    plan = [(lambda ins, n=n: ins[0].at[n], [lambda outs, n=n: outs[n]]) for n in range(2)]
    next_left, next_right = copied("next_rings", plan, CROSS, [both], [CROSS, CROSS])

    def chunk(dz, places, left, right, after):
        at = [(RING[a], RING[b]) for a, b in places]
        nodes = jnp.stack(
            [((x + dx) % SX * SZ + (z + dz) % SZ) * SY + (y + dy) % SY for dy, dx in at]
        )
        order = jnp.stack([(x + dx) % SX * SY + (y + dy) % SY for dy, dx in at])
        meta = jnp.concatenate(
            [
                pattern[nodes].reshape(-1),
                jnp.stack([node * (ROWS // B), pole]),
                jnp.array(places, jnp.int32).reshape(-1),
            ]
        ).astype(jnp.int32)
        keep, give = columns_of(
            places, dz == 0, left, right, meta, root_inverse, diagonal_inverse[0, 0], after
        )
        return keep, give, order.astype(jnp.int32)

    def swapped(give, *after):
        return lax.ppermute(ordered(give, *after), "pole", CORE)

    own_keep, own_give, own_order = chunk(0, ALL, left, right, (next_left,))
    left, right, halves = crossed(next_left, next_right)
    own_got = swapped(own_give, halves[0])
    (own_away,) = pair_sums((1,), coef, own_keep, own_got, ())
    own_far = lax.ppermute(own_away, "pole", Z_HI)
    inner_keep, inner_give, inner = chunk(1, INNER, left, right, (own_away,))
    outer_keep, outer_give, outer = chunk(1, OUTER, left, right, (inner_give,))
    inner_got = swapped(inner_give, own_far, outer_give)
    outer_got = swapped(outer_give, own_far)
    sums = own_sums(coef, own_order, own_keep, own_got, own_far)
    own = in_plane(sums)
    pairs = [
        pair_sums((0, 1), coef, inner_keep, inner_got, (sums,)),
        pair_sums((0, 1), coef, outer_keep, outer_got, ()),
    ]
    (near, away), outer_pair = [
        (send(near, dz=1), lax.ppermute(away, ("pole", "snode"), across()))
        for near, away in pairs
    ]
    inner_pair = (ordered(near, own), away)
    other = in_plane(next_sums(jnp.concatenate([inner, outer]), [inner_pair, outer_pair]))
    rows_out, diag_out = placed(jnp.stack([z, 1 - z]).astype(jnp.int32), own, other)
    return rows_out[:, None], diag_out[:, None]


def solution(mesh):
    in_specs = (
        P("pole", None, None, "snode", None),
        P("pole", "snode", None, None, None),
        P("pole", "snode", None, None, None),
        P(),
        P("pole", None),
        P("pole", None),
    )
    out_specs = (P(None, "snode", None, "pole", None), P(None, "snode", "pole", None))
    return jax.shard_map(
        on_device, mesh=mesh, in_specs=in_specs, out_specs=out_specs, check_vma=False
    )
```

```python
import jax
import jax.numpy as jnp
from jax import lax
from jax.experimental import pallas as pl
from jax.experimental.pallas import tpu as pltpu
from jax.sharding import PartitionSpec as P

B = 128
M = 8
ROWS = 384
PART = 96
DIAG = 32
SX, SZ, SY = 4, 2, 4
COST = pl.CostEstimate(flops=0, bytes_accessed=1, transcendentals=0)
AHEAD = 4
RING = (0, 1, -1, 2)
CORE = [(p, p ^ 1) for p in range(4)]
Z_HI = [(p, p ^ 2) for p in range(4)]
PLANES = [[(x * SZ + z) * SY + y for x in range(SX) for y in range(SY)] for z in range(SZ)]
ALL = [(a, b) for a in range(4) for b in range(4)]
INNER = [(a, b) for a in range(3) for b in range(3)]
OUTER = [(a, 3) for a in range(4)] + [(3, b) for b in range(3)]


def shift(dx=0, dz=0, dy=0):
    return [
        (
            (x * SZ + z) * SY + y,
            (((x + dx) % SX) * SZ + (z + dz) % SZ) * SY + (y + dy) % SY,
        )
        for x in range(SX)
        for z in range(SZ)
        for y in range(SY)
    ]


def across():
    nodes = SX * SZ * SY
    return [
        (p * nodes + a, (p ^ 2) * nodes + b) for p in range(4) for a, b in shift(dz=1)
    ]


def send(value, **by):
    return lax.ppermute(value, "snode", shift(**by))


def ordered(value, *after):
    return pl.pallas_call(
        lambda *refs: None,
        out_shape=jax.ShapeDtypeStruct(value.shape, value.dtype),
        in_specs=[pl.BlockSpec(memory_space=pl.ANY)] * (1 + len(after)),
        out_specs=pl.BlockSpec(memory_space=pl.ANY),
        input_output_aliases={0: 0},
        compiler_params=pltpu.CompilerParams(vmem_limit_bytes=2**20),
        cost_estimate=COST,
        name="ordered",
    )(value, *after)


def copies_body(plan, n_in, n_out, *refs):
    ins, outs = refs[:n_in], refs[n_in : n_in + n_out]
    stages, sems = refs[n_in + n_out : -1], refs[-1]
    first, second = [], []
    for n, (source, targets) in enumerate(plan):
        first.append(pltpu.make_async_copy(source(ins), stages[n], sems.at[n]))
        first[-1].start()
    for n, (source, targets) in enumerate(plan):
        first[n].wait()
        for target in targets:
            at = len(plan) + len(second)
            second.append(pltpu.make_async_copy(stages[n], target(outs), sems.at[at]))
            second[-1].start()
    for copy in second:
        copy.wait()


def copied(name, plan, piece, arrays, shapes):
    n_copies = len(plan) + sum(len(targets) for _, targets in plan)
    return pl.pallas_call(
        lambda *refs: copies_body(plan, len(arrays), len(shapes), *refs),
        out_shape=[jax.ShapeDtypeStruct(shape, jnp.bfloat16) for shape in shapes],
        in_specs=[pl.BlockSpec(memory_space=pl.ANY)] * len(arrays),
        out_specs=[pl.BlockSpec(memory_space=pltpu.HBM)] * len(shapes),
        scratch_shapes=[pltpu.VMEM(piece, jnp.bfloat16)] * len(plan)
        + [pltpu.SemaphoreType.DMA((n_copies,))],
        compiler_params=pltpu.CompilerParams(vmem_limit_bytes=8 * 2**20),
        cost_estimate=COST,
        name=name,
    )(*arrays)


CROSS = (2, 4, 2, 2 * B, B)


def own_rings(factor):
    parts = factor.reshape(2, 2, 2, 2 * B, B).transpose(1, 2, 0, 3, 4)
    arrays = [parts[0]] + [send(parts[0], dx=-d) for d in RING[1:]]
    arrays += [parts[1]] + [send(parts[1], dy=-d) for d in RING[1:]]
    plan = []
    for n in range(8):
        side, at = n // 4, n % 4
        targets = [
            lambda outs, s=side, at=at: outs[s].at[:, at],
            lambda outs, s=side, at=at: outs[2].at[s, :, at],
        ]
        plan.append((lambda ins, n=n: ins[n], targets))
    return copied("own_rings", plan, CROSS[:1] + CROSS[2:], arrays, [CROSS, CROSS, (2,) + CROSS])


def crossed(left, right):
    found = [
        (send(left, dy=-1), send(left, dy=1)),
        (send(right, dx=-1), send(right, dx=1)),
    ]
    arrays = [*found[0], *found[1]]
    plan = [
        (lambda ins, n=n: ins[n].at[1 - n % 2], [lambda outs, n=n: outs[n]]) for n in range(4)
    ]
    halves = copied("halves", plan, CROSS[1:], arrays, [CROSS[1:]] * 4)
    far = [
        (send(halves[1], dy=1), send(halves[0], dy=-1)),
        (send(halves[3], dx=1), send(halves[2], dx=-1)),
    ]
    return [left, *found[0], *far[0]], [right, *found[1], *far[1]], halves


def factor_copies(places, left, right, factors):
    dys = sorted({a for a, _ in places})
    dxs = sorted({b for _, b in places})
    found = []
    for side, ours, others in ((1, dxs, dys), (0, dys, dxs)):
        sources = (left, right)[side]
        for one in ours:
            far = [o for o in others if ((o, one) if side else (one, o)) in places]
            span = pl.ds(far[0], len(far))
            for h in range(2):
                ref = sources[one].at[h, span] if one < 3 else sources[3 + h].at[span]
                if side:
                    found.append((ref, factors.at[span, one, 2 + h]))
                else:
                    found.append((ref, factors.at[one, span, h]))
    return found


def column_body(places, with_own, meta, root, diag_inv, *refs):
    count = len(places)
    n_side = 3 if places is INNER else 5
    left, right = refs[:n_side], refs[n_side : 2 * n_side]
    keep, give, blocks, factors, column, total, root_sems, sems = refs[-8:]

    def fetch(j, i):
        slot = j % AHEAD
        for h in range(2):
            pltpu.make_async_copy(
                root.at[0, h, meta[j * M + i]],
                blocks.at[slot, i, :, pl.ds(h * B, B)],
                root_sems.at[slot],
            ).start()

    copies = [
        pltpu.make_async_copy(source, target, sems.at[n])
        for n, (source, target) in enumerate(factor_copies(places, left, right, factors))
    ]
    for copy in copies:
        copy.start()

    @pl.loop(0, (AHEAD - 1) * M)
    def _(n):
        fetch(n // M, n % M)

    for copy in copies:
        copy.wait()
    first_block = meta[count * M]
    pole = meta[count * M + 1]

    @pl.loop(0, count)
    def _(j):
        @pl.when(j + AHEAD - 1 < count)
        def _():
            for i in range(M):
                fetch(j + AHEAD - 1, i)

        dy = meta[count * M + 2 + 2 * j]
        dx = meta[count * M + 3 + 2 * j]
        slot = j % AHEAD

        pltpu.make_async_copy(blocks.at[slot], blocks.at[slot], root_sems.at[slot]).wait()

        product = None
        for i in range(M):
            at = pl.ds((i % 2) * B, B)
            real, imag = factors[dy, dx, i // 2, 0, at, :], factors[dy, dx, i // 2, 1, at, :]
            weights = jnp.concatenate(
                [
                    jnp.concatenate([real, imag], axis=1),
                    jnp.concatenate([-imag, real], axis=1),
                ],
                axis=0,
            )
            term = jnp.dot(blocks[slot, i], weights, preferred_element_type=jnp.float32)
            product = term if product is None else product + term
        column[...] = (-product).astype(jnp.bfloat16)
        total[...] = jnp.zeros_like(total)

        @pl.loop(0, M)
        def _(i):
            local = meta[j * M + i] - first_block

            @pl.when((local >= 0) & (local < ROWS // B))
            def _():
                rows = column[pl.ds(pl.multiple_of(local * B, B), B), :]
                real, imag = rows[:, :B], rows[:, B:]
                values = jnp.concatenate(
                    [
                        jnp.concatenate([real, imag], axis=1),
                        jnp.concatenate([-imag, real], axis=1),
                    ],
                    axis=0,
                )
                at = pl.ds(pl.multiple_of((i % 2) * B, B), B)
                factor = jnp.concatenate(
                    [factors[dy, dx, i // 2, 0, at, :], factors[dy, dx, i // 2, 1, at, :]], axis=0
                )
                total[...] += lax.dot_general(
                    factor, values, (((0,), (0,)), ((), ())), preferred_element_type=jnp.float32
                )

        if with_own:

            @pl.when(j == 0)
            def _():
                total[:, :B] -= diag_inv[0].astype(jnp.float32)
                total[:, B:] -= diag_inv[1].astype(jnp.float32)

        for n in range(4):
            out, e = (keep, give)[n >> 1], n & 1
            part = pole ^ ((e << 1) | (n >> 1))
            rows_at = pl.multiple_of(part * PART, PART)
            diag_at = pl.multiple_of(part * DIAG, DIAG)
            for h in range(2):
                lanes = slice(h * B, (h + 1) * B)
                out[e, j, h, :PART, :] = column[pl.ds(rows_at, PART), lanes]
                share = -total[pl.ds(diag_at, DIAG), lanes]
                coarse = share.astype(jnp.bfloat16)
                out[e, j, h, PART : PART + DIAG, :] = coarse
                rest = share - coarse.astype(jnp.float32)
                out[e, j, h, PART + DIAG :, :] = rest.astype(jnp.bfloat16)


def columns_of(places, with_own, left, right, meta, root, diag_inv, after):
    count = len(places)
    piece = jax.ShapeDtypeStruct((2, count, 2, PART + 2 * DIAG, B), jnp.bfloat16)
    n_copies = 2 * (len({a for a, _ in places}) + len({b for _, b in places}))
    n_side = 3 if places is INNER else 5
    sources = [*left[:n_side], *right[:n_side], *after]
    return pl.pallas_call(
        lambda *refs: column_body(places, with_own, *refs),
        out_shape=[piece] * 2,
        in_specs=[
            pl.BlockSpec(memory_space=pltpu.SMEM),
            pl.BlockSpec(memory_space=pl.ANY),
            pl.BlockSpec(memory_space=pltpu.VMEM),
        ]
        + [pl.BlockSpec(memory_space=pl.ANY)] * len(sources),
        out_specs=[pl.BlockSpec(memory_space=pltpu.VMEM)] * 2,
        scratch_shapes=[
            pltpu.VMEM((AHEAD, M, ROWS, 2 * B), jnp.bfloat16),
            pltpu.VMEM((4, 4, 4, 2, 2 * B, B), jnp.bfloat16),
            pltpu.VMEM((ROWS, 2 * B), jnp.bfloat16),
            pltpu.VMEM((B, 2 * B), jnp.float32),
            pltpu.SemaphoreType.DMA((AHEAD,)),
            pltpu.SemaphoreType.DMA((n_copies,)),
        ],
        compiler_params=pltpu.CompilerParams(vmem_limit_bytes=28 * 2**20),
        cost_estimate=pl.CostEstimate(
            flops=2 * count * ROWS * 2 * M * B * 2 * B,
            bytes_accessed=count * (2 * M * B * B * 2 + 2 * M * ROWS * B * 2),
            transcendentals=0,
        ),
        name="columns",
    )(meta, root, diag_inv, *sources)


def weighted(coef, which, mine, other):
    own_real, own_imag = mine[0].astype(jnp.float32), mine[1].astype(jnp.float32)
    far_real, far_imag = other[0].astype(jnp.float32), other[1].astype(jnp.float32)
    value = (
        coef[0, 2 * which] * own_imag
        + coef[0, 2 * which + 1] * own_real
        + coef[1, 2 * which] * far_imag
        + coef[1, 2 * which + 1] * far_real
    )
    return value[:PART], value[PART : PART + DIAG] + value[PART + DIAG :]


def pair_body(parts, coef, mine, other, *refs):
    outs = refs[-len(parts) :]

    @pl.loop(0, mine.shape[1])
    def _(j):
        for e, out in zip(parts, outs):
            for which in range(2):
                rows, diag = weighted(coef, which, mine[e, j], other[e, j])
                out[j, which, :PART, :] = rows.astype(jnp.bfloat16)
                out[j, which, PART:, :] = diag.astype(jnp.bfloat16)


def pair_sums(parts, coef, mine, other, after):
    count = mine.shape[1]
    return pl.pallas_call(
        lambda *refs: pair_body(parts, *refs),
        out_shape=[jax.ShapeDtypeStruct((count, 2, PART + DIAG, B), jnp.bfloat16)] * len(parts),
        in_specs=[pl.BlockSpec(memory_space=pltpu.SMEM)]
        + [pl.BlockSpec(memory_space=pltpu.VMEM)] * 2
        + [pl.BlockSpec(memory_space=pl.ANY)] * len(after),
        out_specs=[pl.BlockSpec(memory_space=pltpu.VMEM)] * len(parts),
        compiler_params=pltpu.CompilerParams(vmem_limit_bytes=16 * 2**20),
        cost_estimate=COST,
        name="pair_sums",
    )(coef, mine, other, *after)


def own_body(coef, order, mine, other, far, out):
    @pl.loop(0, far.shape[0])
    def _(j):
        at = order[j]
        for which in range(2):
            rows, diag = weighted(coef, which, mine[0, j], other[0, j])
            rows = rows + far[j, which, :PART, :].astype(jnp.float32)
            diag = diag + far[j, which, PART:, :].astype(jnp.float32)
            out[at, which, :PART, :] = rows.astype(jnp.bfloat16)
            out[at, which, PART:, :] = diag.astype(jnp.bfloat16)


def own_sums(coef, order, mine, other, far):
    return pl.pallas_call(
        own_body,
        out_shape=jax.ShapeDtypeStruct(far.shape, jnp.bfloat16),
        in_specs=[pl.BlockSpec(memory_space=pltpu.SMEM)] * 2
        + [pl.BlockSpec(memory_space=pltpu.VMEM)] * 3,
        out_specs=pl.BlockSpec(memory_space=pltpu.VMEM),
        compiler_params=pltpu.CompilerParams(vmem_limit_bytes=16 * 2**20),
        cost_estimate=COST,
        name="own_sums",
    )(coef, order, mine, other, far)


def next_body(order, *refs):
    out, start = refs[-1], 0
    for near, far in zip(refs[:-1:2], refs[1:-1:2]):

        @pl.loop(0, near.shape[0])
        def _(j, start=start, near=near, far=far):
            value = near[j].astype(jnp.float32) + far[j].astype(jnp.float32)
            out[order[start + j]] = value.astype(jnp.bfloat16)

        start += near.shape[0]


def next_sums(order, pairs):
    return pl.pallas_call(
        next_body,
        out_shape=jax.ShapeDtypeStruct((SX * SY, 2, PART + DIAG, B), jnp.bfloat16),
        in_specs=[pl.BlockSpec(memory_space=pltpu.SMEM)]
        + [pl.BlockSpec(memory_space=pltpu.VMEM)] * (2 * len(pairs)),
        out_specs=pl.BlockSpec(memory_space=pltpu.VMEM),
        compiler_params=pltpu.CompilerParams(vmem_limit_bytes=16 * 2**20),
        cost_estimate=COST,
        name="next_sums",
    )(order, *[piece for pair in pairs for piece in pair])


def place_body(plane, own, other, rows_out, diag_out):
    diag_out[...] = jnp.zeros_like(diag_out)
    for n, pieces in enumerate((own, other)):
        z = plane[n]

        @pl.loop(0, SX * SY)
        def _(j, pieces=pieces, z=z):
            owner = (j // SY * SZ + z) * SY + j % SY
            for which in range(2):
                rows_out[which, owner] = pieces[j, which, :PART, :].astype(jnp.float32)
            diag_out[...] += pieces[j, :, PART:, :].astype(jnp.float32)


def placed(plane, own, other):
    return pl.pallas_call(
        place_body,
        out_shape=[
            jax.ShapeDtypeStruct((2, SX * SZ * SY, PART, B), jnp.float32),
            jax.ShapeDtypeStruct((2, DIAG, B), jnp.float32),
        ],
        in_specs=[pl.BlockSpec(memory_space=pltpu.SMEM)]
        + [pl.BlockSpec(memory_space=pltpu.VMEM)] * 2,
        out_specs=[pl.BlockSpec(memory_space=pltpu.VMEM)] * 2,
        compiler_params=pltpu.CompilerParams(vmem_limit_bytes=16 * 2**20),
        name="placed",
    )(plane, own, other)


def in_plane(value):
    return lax.all_to_all(
        value, "snode", split_axis=0, concat_axis=0, axis_index_groups=PLANES, tiled=True
    )


def on_device(root_inverse, factor_columns, diagonal_inverse, pattern, pole_weights, pole_shifts):
    node = lax.axis_index("snode")
    pole = lax.axis_index("pole")
    x, z, y = node // (SZ * SY), (node // SY) % SZ, node % SY
    weight_real, weight_imag = pole_weights[0, 0], pole_weights[0, 1]
    shift_real, shift_imag = pole_shifts[0, 0], pole_shifts[0, 1]
    own_coef = jnp.stack(
        [
            weight_real,
            weight_imag,
            weight_real * shift_real - weight_imag * shift_imag,
            weight_real * shift_imag + weight_imag * shift_real,
        ]
    )[None]
    coef = jnp.concatenate([own_coef, lax.ppermute(own_coef, "pole", CORE)])
    left, right, both = own_rings(factor_columns[0, 0])
    both = send(both, dz=1)
    left, right, _ = crossed(left, right)
    plan = [(lambda ins, n=n: ins[0].at[n], [lambda outs, n=n: outs[n]]) for n in range(2)]
    next_left, next_right = copied("next_rings", plan, CROSS, [both], [CROSS, CROSS])

    def chunk(dz, places, left, right, after):
        at = [(RING[a], RING[b]) for a, b in places]
        nodes = jnp.stack(
            [((x + dx) % SX * SZ + (z + dz) % SZ) * SY + (y + dy) % SY for dy, dx in at]
        )
        order = jnp.stack([(x + dx) % SX * SY + (y + dy) % SY for dy, dx in at])
        meta = jnp.concatenate(
            [
                pattern[nodes].reshape(-1),
                jnp.stack([node * (ROWS // B), pole]),
                jnp.array(places, jnp.int32).reshape(-1),
            ]
        ).astype(jnp.int32)
        keep, give = columns_of(
            places, dz == 0, left, right, meta, root_inverse, diagonal_inverse[0, 0], after
        )
        return keep, give, order.astype(jnp.int32)

    def swapped(give, *after):
        return lax.ppermute(ordered(give, *after), "pole", CORE)

    own_keep, own_give, own_order = chunk(0, ALL, left, right, (next_left,))
    left, right, halves = crossed(next_left, next_right)
    own_got = swapped(own_give, halves[0])
    (own_away,) = pair_sums((1,), coef, own_keep, own_got, ())
    own_far = lax.ppermute(own_away, "pole", Z_HI)
    inner_keep, inner_give, inner = chunk(1, INNER, left, right, (own_away,))
    outer_keep, outer_give, outer = chunk(1, OUTER, left, right, (inner_give,))
    inner_got = swapped(inner_give, own_far, outer_give)
    outer_got = swapped(outer_give, own_far)
    sums = own_sums(coef, own_order, own_keep, own_got, own_far)
    own = in_plane(sums)
    pairs = [
        pair_sums((0, 1), coef, inner_keep, inner_got, (sums,)),
        pair_sums((0, 1), coef, outer_keep, outer_got, ()),
    ]
    (near, away), outer_pair = [
        (send(near, dz=1), lax.ppermute(away, ("pole", "snode"), across()))
        for near, away in pairs
    ]
    inner_pair = (ordered(near, own), away)
    other = in_plane(next_sums(jnp.concatenate([inner, outer]), [inner_pair, outer_pair]))
    rows_out, diag_out = placed(jnp.stack([z, 1 - z]).astype(jnp.int32), own, other)
    return rows_out[:, None], diag_out[:, None]


def solution(mesh):
    in_specs = (
        P("pole", None, None, "snode", None),
        P("pole", "snode", None, None, None),
        P("pole", "snode", None, None, None),
        P(),
        P("pole", None),
        P("pole", None),
    )
    out_specs = (P(None, "snode", None, "pole", None), P(None, "snode", "pole", None))
    return jax.shard_map(
        on_device, mesh=mesh, in_specs=in_specs, out_specs=out_specs, check_vma=False
    )
```

```python
import jax
import jax.numpy as jnp
from jax import lax
from jax.experimental import pallas as pl
from jax.experimental.pallas import tpu as pltpu
from jax.sharding import PartitionSpec as P

B = 128
M = 8
ROWS = 384
PART = 96
DIAG = 32
SX, SZ, SY = 4, 2, 4
COST = pl.CostEstimate(flops=0, bytes_accessed=1, transcendentals=0)
AHEAD = 4
RING = (0, 1, -1, 2)
CORE = [(p, p ^ 1) for p in range(4)]
Z_HI = [(p, p ^ 2) for p in range(4)]
PLANES = [[(x * SZ + z) * SY + y for x in range(SX) for y in range(SY)] for z in range(SZ)]
ALL = [(a, b) for a in range(4) for b in range(4)]
INNER = [(a, b) for a in range(3) for b in range(3)]
OUTER = [(a, 3) for a in range(4)] + [(3, b) for b in range(3)]


def shift(dx=0, dz=0, dy=0):
    return [
        (
            (x * SZ + z) * SY + y,
            (((x + dx) % SX) * SZ + (z + dz) % SZ) * SY + (y + dy) % SY,
        )
        for x in range(SX)
        for z in range(SZ)
        for y in range(SY)
    ]


def across():
    nodes = SX * SZ * SY
    return [
        (p * nodes + a, (p ^ 2) * nodes + b) for p in range(4) for a, b in shift(dz=1)
    ]


def send(value, **by):
    return lax.ppermute(value, "snode", shift(**by))


def ordered(value, *after):
    return pl.pallas_call(
        lambda *refs: None,
        out_shape=jax.ShapeDtypeStruct(value.shape, value.dtype),
        in_specs=[pl.BlockSpec(memory_space=pl.ANY)] * (1 + len(after)),
        out_specs=pl.BlockSpec(memory_space=pl.ANY),
        input_output_aliases={0: 0},
        compiler_params=pltpu.CompilerParams(vmem_limit_bytes=2**20),
        cost_estimate=COST,
        name="ordered",
    )(value, *after)


def copies_body(plan, n_in, n_out, *refs):
    ins, outs = refs[:n_in], refs[n_in : n_in + n_out]
    stages, sems = refs[n_in + n_out : -1], refs[-1]
    first, second = [], []
    for n, (source, targets) in enumerate(plan):
        first.append(pltpu.make_async_copy(source(ins), stages[n], sems.at[n]))
        first[-1].start()
    for n, (source, targets) in enumerate(plan):
        first[n].wait()
        for target in targets:
            at = len(plan) + len(second)
            second.append(pltpu.make_async_copy(stages[n], target(outs), sems.at[at]))
            second[-1].start()
    for copy in second:
        copy.wait()


def copied(name, plan, piece, arrays, shapes):
    n_copies = len(plan) + sum(len(targets) for _, targets in plan)
    return pl.pallas_call(
        lambda *refs: copies_body(plan, len(arrays), len(shapes), *refs),
        out_shape=[jax.ShapeDtypeStruct(shape, jnp.bfloat16) for shape in shapes],
        in_specs=[pl.BlockSpec(memory_space=pl.ANY)] * len(arrays),
        out_specs=[pl.BlockSpec(memory_space=pltpu.HBM)] * len(shapes),
        scratch_shapes=[pltpu.VMEM(piece, jnp.bfloat16)] * len(plan)
        + [pltpu.SemaphoreType.DMA((n_copies,))],
        compiler_params=pltpu.CompilerParams(vmem_limit_bytes=8 * 2**20),
        cost_estimate=COST,
        name=name,
    )(*arrays)


CROSS = (2, 4, 2, 2 * B, B)


def own_rings(factor, after):
    parts = factor.reshape(2, 2, 2, 2 * B, B).transpose(1, 2, 0, 3, 4)
    arrays = [parts[0]] + [send(parts[0], dx=-d) for d in RING[1:]]
    arrays += [parts[1]] + [send(parts[1], dy=-d) for d in RING[1:]]
    plan = []
    for n in range(8):
        side, at = n // 4, n % 4
        targets = [
            lambda outs, s=side, at=at: outs[s].at[:, at],
            lambda outs, s=side, at=at: outs[2].at[s, :, at],
        ]
        plan.append((lambda ins, n=n: ins[n], targets))
    return copied("own_rings", plan, CROSS[:1] + CROSS[2:], [*arrays, after], [CROSS, CROSS, (2,) + CROSS])


def crossed(left, right):
    found = [
        (send(left, dy=-1), send(left, dy=1)),
        (send(right, dx=-1), send(right, dx=1)),
    ]
    arrays = [*found[0], *found[1]]
    plan = [
        (lambda ins, n=n: ins[n].at[1 - n % 2], [lambda outs, n=n: outs[n]]) for n in range(4)
    ]
    halves = copied("halves", plan, CROSS[1:], arrays, [CROSS[1:]] * 4)
    far = [
        (send(halves[1], dy=1), send(halves[0], dy=-1)),
        (send(halves[3], dx=1), send(halves[2], dx=-1)),
    ]
    return [left, *found[0], *far[0]], [right, *found[1], *far[1]], halves


def factor_copies(places, left, right, factors):
    dys = sorted({a for a, _ in places})
    dxs = sorted({b for _, b in places})
    found = []
    for side, ours, others in ((1, dxs, dys), (0, dys, dxs)):
        sources = (left, right)[side]
        for one in ours:
            far = [o for o in others if ((o, one) if side else (one, o)) in places]
            span = pl.ds(far[0], len(far))
            for h in range(2):
                ref = sources[one].at[h, span] if one < 3 else sources[3 + h].at[span]
                if side:
                    found.append((ref, factors.at[span, one, 2 + h]))
                else:
                    found.append((ref, factors.at[one, span, h]))
    return found


def column_body(places, with_own, meta, root, diag_inv, *refs):
    count = len(places)
    n_side = 3 if places is INNER else 5
    left, right = refs[:n_side], refs[n_side : 2 * n_side]
    keep, give, blocks, factors, column, total, root_sems, sems = refs[-8:]

    def fetch(j, i):
        slot = j % AHEAD
        for h in range(2):
            pltpu.make_async_copy(
                root.at[0, h, meta[j * M + i]],
                blocks.at[slot, i, :, pl.ds(h * B, B)],
                root_sems.at[slot],
            ).start()

    copies = [
        pltpu.make_async_copy(source, target, sems.at[n])
        for n, (source, target) in enumerate(factor_copies(places, left, right, factors))
    ]
    for copy in copies:
        copy.start()

    @pl.loop(0, (AHEAD - 1) * M)
    def _(n):
        fetch(n // M, n % M)

    for copy in copies:
        copy.wait()
    first_block = meta[count * M]
    pole = meta[count * M + 1]

    @pl.loop(0, count)
    def _(j):
        @pl.when(j + AHEAD - 1 < count)
        def _():
            for i in range(M):
                fetch(j + AHEAD - 1, i)

        dy = meta[count * M + 2 + 2 * j]
        dx = meta[count * M + 3 + 2 * j]
        slot = j % AHEAD

        pltpu.make_async_copy(blocks.at[slot], blocks.at[slot], root_sems.at[slot]).wait()

        product = None
        for i in range(M):
            at = pl.ds((i % 2) * B, B)
            real, imag = factors[dy, dx, i // 2, 0, at, :], factors[dy, dx, i // 2, 1, at, :]
            weights = jnp.concatenate(
                [
                    jnp.concatenate([real, imag], axis=1),
                    jnp.concatenate([-imag, real], axis=1),
                ],
                axis=0,
            )
            term = jnp.dot(blocks[slot, i], weights, preferred_element_type=jnp.float32)
            product = term if product is None else product + term
        column[...] = (-product).astype(jnp.bfloat16)
        total[...] = jnp.zeros_like(total)

        @pl.loop(0, M)
        def _(i):
            local = meta[j * M + i] - first_block

            @pl.when((local >= 0) & (local < ROWS // B))
            def _():
                rows = column[pl.ds(pl.multiple_of(local * B, B), B), :]
                real, imag = rows[:, :B], rows[:, B:]
                values = jnp.concatenate(
                    [
                        jnp.concatenate([real, imag], axis=1),
                        jnp.concatenate([-imag, real], axis=1),
                    ],
                    axis=0,
                )
                at = pl.ds(pl.multiple_of((i % 2) * B, B), B)
                factor = jnp.concatenate(
                    [factors[dy, dx, i // 2, 0, at, :], factors[dy, dx, i // 2, 1, at, :]], axis=0
                )
                total[...] += lax.dot_general(
                    factor, values, (((0,), (0,)), ((), ())), preferred_element_type=jnp.float32
                )

        if with_own:

            @pl.when(j == 0)
            def _():
                total[:, :B] -= diag_inv[0].astype(jnp.float32)
                total[:, B:] -= diag_inv[1].astype(jnp.float32)

        for n in range(4):
            out, e = (keep, give)[n >> 1], n & 1
            part = pole ^ ((e << 1) | (n >> 1))
            rows_at = pl.multiple_of(part * PART, PART)
            diag_at = pl.multiple_of(part * DIAG, DIAG)
            for h in range(2):
                lanes = slice(h * B, (h + 1) * B)
                out[e, j, h, :PART, :] = column[pl.ds(rows_at, PART), lanes]
                share = -total[pl.ds(diag_at, DIAG), lanes]
                coarse = share.astype(jnp.bfloat16)
                out[e, j, h, PART : PART + DIAG, :] = coarse
                rest = share - coarse.astype(jnp.float32)
                out[e, j, h, PART + DIAG :, :] = rest.astype(jnp.bfloat16)


def columns_of(places, with_own, left, right, meta, root, diag_inv, after):
    count = len(places)
    piece = jax.ShapeDtypeStruct((2, count, 2, PART + 2 * DIAG, B), jnp.bfloat16)
    n_copies = 2 * (len({a for a, _ in places}) + len({b for _, b in places}))
    n_side = 3 if places is INNER else 5
    sources = [*left[:n_side], *right[:n_side], *after]
    return pl.pallas_call(
        lambda *refs: column_body(places, with_own, *refs),
        out_shape=[piece] * 2,
        in_specs=[
            pl.BlockSpec(memory_space=pltpu.SMEM),
            pl.BlockSpec(memory_space=pl.ANY),
            pl.BlockSpec(memory_space=pltpu.VMEM),
        ]
        + [pl.BlockSpec(memory_space=pl.ANY)] * len(sources),
        out_specs=[pl.BlockSpec(memory_space=pltpu.VMEM)] * 2,
        scratch_shapes=[
            pltpu.VMEM((AHEAD, M, ROWS, 2 * B), jnp.bfloat16),
            pltpu.VMEM((4, 4, 4, 2, 2 * B, B), jnp.bfloat16),
            pltpu.VMEM((ROWS, 2 * B), jnp.bfloat16),
            pltpu.VMEM((B, 2 * B), jnp.float32),
            pltpu.SemaphoreType.DMA((AHEAD,)),
            pltpu.SemaphoreType.DMA((n_copies,)),
        ],
        compiler_params=pltpu.CompilerParams(vmem_limit_bytes=60 * 2**20),
        cost_estimate=pl.CostEstimate(
            flops=2 * count * ROWS * 2 * M * B * 2 * B,
            bytes_accessed=count * (2 * M * B * B * 2 + 2 * M * ROWS * B * 2),
            transcendentals=0,
        ),
        name="columns",
    )(meta, root, diag_inv, *sources)


def weighted(coef, which, mine, other):
    own_real, own_imag = mine[0].astype(jnp.float32), mine[1].astype(jnp.float32)
    far_real, far_imag = other[0].astype(jnp.float32), other[1].astype(jnp.float32)
    value = (
        coef[0, 2 * which] * own_imag
        + coef[0, 2 * which + 1] * own_real
        + coef[1, 2 * which] * far_imag
        + coef[1, 2 * which + 1] * far_real
    )
    return value[:PART], value[PART : PART + DIAG] + value[PART + DIAG :]


def pair_body(parts, coef, mine, other, *refs):
    outs = refs[-len(parts) :]

    @pl.loop(0, mine.shape[1])
    def _(j):
        for e, out in zip(parts, outs):
            for which in range(2):
                rows, diag = weighted(coef, which, mine[e, j], other[e, j])
                out[j, which, :PART, :] = rows.astype(jnp.bfloat16)
                out[j, which, PART:, :] = diag.astype(jnp.bfloat16)


def pair_sums(parts, coef, mine, other, after):
    count = mine.shape[1]
    return pl.pallas_call(
        lambda *refs: pair_body(parts, *refs),
        out_shape=[jax.ShapeDtypeStruct((count, 2, PART + DIAG, B), jnp.bfloat16)] * len(parts),
        in_specs=[pl.BlockSpec(memory_space=pltpu.SMEM)]
        + [pl.BlockSpec(memory_space=pltpu.VMEM)] * 2
        + [pl.BlockSpec(memory_space=pl.ANY)] * len(after),
        out_specs=[pl.BlockSpec(memory_space=pltpu.VMEM)] * len(parts),
        compiler_params=pltpu.CompilerParams(vmem_limit_bytes=16 * 2**20),
        cost_estimate=COST,
        name="pair_sums",
    )(coef, mine, other, *after)


def own_body(coef, order, mine, other, far, out):
    @pl.loop(0, far.shape[0])
    def _(j):
        at = order[j]
        for which in range(2):
            rows, diag = weighted(coef, which, mine[0, j], other[0, j])
            rows = rows + far[j, which, :PART, :].astype(jnp.float32)
            diag = diag + far[j, which, PART:, :].astype(jnp.float32)
            out[at, which, :PART, :] = rows.astype(jnp.bfloat16)
            out[at, which, PART:, :] = diag.astype(jnp.bfloat16)


def own_sums(coef, order, mine, other, far):
    return pl.pallas_call(
        own_body,
        out_shape=jax.ShapeDtypeStruct(far.shape, jnp.bfloat16),
        in_specs=[pl.BlockSpec(memory_space=pltpu.SMEM)] * 2
        + [pl.BlockSpec(memory_space=pltpu.VMEM)] * 3,
        out_specs=pl.BlockSpec(memory_space=pltpu.VMEM),
        compiler_params=pltpu.CompilerParams(vmem_limit_bytes=16 * 2**20),
        cost_estimate=COST,
        name="own_sums",
    )(coef, order, mine, other, far)


def next_body(order, *refs):
    out, start = refs[-1], 0
    for near, far in zip(refs[:-1:2], refs[1:-1:2]):

        @pl.loop(0, near.shape[0])
        def _(j, start=start, near=near, far=far):
            value = near[j].astype(jnp.float32) + far[j].astype(jnp.float32)
            out[order[start + j]] = value.astype(jnp.bfloat16)

        start += near.shape[0]


def next_sums(order, pairs):
    return pl.pallas_call(
        next_body,
        out_shape=jax.ShapeDtypeStruct((SX * SY, 2, PART + DIAG, B), jnp.bfloat16),
        in_specs=[pl.BlockSpec(memory_space=pltpu.SMEM)]
        + [pl.BlockSpec(memory_space=pltpu.VMEM)] * (2 * len(pairs)),
        out_specs=pl.BlockSpec(memory_space=pltpu.VMEM),
        compiler_params=pltpu.CompilerParams(vmem_limit_bytes=16 * 2**20),
        cost_estimate=COST,
        name="next_sums",
    )(order, *[piece for pair in pairs for piece in pair])


def place_body(plane, own, other, rows_out, diag_out):
    diag_out[...] = jnp.zeros_like(diag_out)
    for n, pieces in enumerate((own, other)):
        z = plane[n]

        @pl.loop(0, SX * SY)
        def _(j, pieces=pieces, z=z):
            owner = (j // SY * SZ + z) * SY + j % SY
            for which in range(2):
                rows_out[which, owner] = pieces[j, which, :PART, :].astype(jnp.float32)
            diag_out[...] += pieces[j, :, PART:, :].astype(jnp.float32)


def placed(plane, own, other):
    return pl.pallas_call(
        place_body,
        out_shape=[
            jax.ShapeDtypeStruct((2, SX * SZ * SY, PART, B), jnp.float32),
            jax.ShapeDtypeStruct((2, DIAG, B), jnp.float32),
        ],
        in_specs=[pl.BlockSpec(memory_space=pltpu.SMEM)]
        + [pl.BlockSpec(memory_space=pltpu.VMEM)] * 2,
        out_specs=[pl.BlockSpec(memory_space=pltpu.VMEM)] * 2,
        compiler_params=pltpu.CompilerParams(vmem_limit_bytes=16 * 2**20),
        name="placed",
    )(plane, own, other)


def in_plane(value):
    return lax.all_to_all(
        value, "snode", split_axis=0, concat_axis=0, axis_index_groups=PLANES, tiled=True
    )


def on_device(root_inverse, factor_columns, diagonal_inverse, pattern, pole_weights, pole_shifts):
    node = lax.axis_index("snode")
    pole = lax.axis_index("pole")
    x, z, y = node // (SZ * SY), (node // SY) % SZ, node % SY
    weight_real, weight_imag = pole_weights[0, 0], pole_weights[0, 1]
    shift_real, shift_imag = pole_shifts[0, 0], pole_shifts[0, 1]
    own_coef = jnp.stack(
        [
            weight_real,
            weight_imag,
            weight_real * shift_real - weight_imag * shift_imag,
            weight_real * shift_imag + weight_imag * shift_real,
        ]
    )[None]
    coef = jnp.concatenate([own_coef, lax.ppermute(own_coef, "pole", CORE)])
    left, right, both = own_rings(factor_columns[0, 0], coef)
    both = send(both, dz=1)
    left, right, _ = crossed(left, right)
    plan = [(lambda ins, n=n: ins[0].at[n], [lambda outs, n=n: outs[n]]) for n in range(2)]
    next_left, next_right = copied("next_rings", plan, CROSS, [both], [CROSS, CROSS])

    def chunk(dz, places, left, right, after):
        at = [(RING[a], RING[b]) for a, b in places]
        nodes = jnp.stack(
            [((x + dx) % SX * SZ + (z + dz) % SZ) * SY + (y + dy) % SY for dy, dx in at]
        )
        order = jnp.stack([(x + dx) % SX * SY + (y + dy) % SY for dy, dx in at])
        meta = jnp.concatenate(
            [
                pattern[nodes].reshape(-1),
                jnp.stack([node * (ROWS // B), pole]),
                jnp.array(places, jnp.int32).reshape(-1),
            ]
        ).astype(jnp.int32)
        keep, give = columns_of(
            places, dz == 0, left, right, meta, root_inverse, diagonal_inverse[0, 0], after
        )
        return keep, give, order.astype(jnp.int32)

    def swapped(give, *after):
        return lax.ppermute(ordered(give, *after), "pole", CORE)

    own_keep, own_give, own_order = chunk(0, ALL, left, right, (next_left,))
    left, right, halves = crossed(next_left, next_right)
    own_got = swapped(own_give, halves[0])
    (own_away,) = pair_sums((1,), coef, own_keep, own_got, ())
    own_far = lax.ppermute(own_away, "pole", Z_HI)
    inner_keep, inner_give, inner = chunk(1, INNER, left, right, (own_away,))
    outer_keep, outer_give, outer = chunk(1, OUTER, left, right, (inner_give,))
    inner_got = swapped(inner_give, own_far, outer_give)
    outer_got = swapped(outer_give, own_far)
    sums = own_sums(coef, own_order, own_keep, own_got, own_far)
    own = in_plane(sums)
    pairs = [
        pair_sums((0, 1), coef, inner_keep, inner_got, (sums,)),
        pair_sums((0, 1), coef, outer_keep, outer_got, ()),
    ]
    (near, away), outer_pair = [
        (send(near, dz=1), lax.ppermute(away, ("pole", "snode"), across()))
        for near, away in pairs
    ]
    inner_pair = (ordered(near, own), away)
    other = in_plane(next_sums(jnp.concatenate([inner, outer]), [inner_pair, outer_pair]))
    rows_out, diag_out = placed(jnp.stack([z, 1 - z]).astype(jnp.int32), own, other)
    return rows_out[:, None], diag_out[:, None]


def solution(mesh):
    in_specs = (
        P("pole", None, None, "snode", None),
        P("pole", "snode", None, None, None),
        P("pole", "snode", None, None, None),
        P(),
        P("pole", None),
        P("pole", None),
    )
    out_specs = (P(None, "snode", None, "pole", None), P(None, "snode", "pole", None))
    return jax.shard_map(
        on_device, mesh=mesh, in_specs=in_specs, out_specs=out_specs, check_vma=False
    )
```
